128 devices in a mesh: sp: 8 (over x, core), ep: 16 (over z, y).
Axes of the slice: x: 4, y: 4, z: 4, core: 2. Of those that a mesh axis runs over, the one named last changes fastest.
Arguments:
- latent: bfloat16 [16, 1024, 4096], P('ep', 'sp'), may hold values from -36 to 36
- attention_in: bfloat16 [16, 1024, 3, 4096], P('ep', 'sp'), may hold values from -6 to 6
- out_weight: bfloat16 [4096, 4096], P('sp'), may hold values from -0.09375 to 0.09375
- modulation: float32 [4, 4096], replicated, may hold values from -4 to 4
- route_experts: int32 [16, 1024, 2], P('ep', 'sp'), may hold values from 0 to 31, as said below
- route_slots: int32 [16, 1024, 2], P('ep', 'sp'), may hold values from 0 to 11, as said below
- route_gates: float32 [16, 1024, 2], P('ep', 'sp'), may hold values from 0.1 to 1
- gate_weight: bfloat16 [16, 4096, 4096], P('ep', None, 'sp'), may hold values from -0.09375 to 0.09375
- up_weight: bfloat16 [16, 4096, 4096], P('ep', None, 'sp'), may hold values from -0.09375 to 0.09375
- down_weight: bfloat16 [16, 4096, 4096], P('ep', 'sp'), may hold values from -0.125 to 0.125
Outputs:
- block_out: bfloat16 [16, 1024, 4096], P('ep', 'sp')
The draws below stay inside these ranges and needn't reach their ends.
Inputs may be any that keep to these rules, and one draw needn't show every extreme that they name: `route_experts`: each token names two different experts. Among the 128 tokens of one device block no expert is named more than 12 times; in every device block some expert is named exactly 12 times, and one expert is named exactly 12 times in every device block. `route_slots`: the routes of one device block to one expert hold distinct slots.
All inputs are finite; a program needn't handle non-finite values.
Results may differ from the reference program's by a relative error of at most 0.013.
Values may be sent and summed in bfloat16 or wider, within the bound.
A program may use at most 192 MiB of HBM per device.

```python
import math
import jax
import jax.numpy as jnp
from jax import lax

D = 4096
HD = 128
FF = 2048
TOK_DEV = 128
EXPERTS = 32
WINDOWS = 16
WIN_TOK = 1024
GROUP_HEADS = 4
SHARDS = 4
SHARD_FF = 512
CAP = 12
N_SP = 8


def route_tables(key):
    block_count = WINDOWS * (WIN_TOK // TOK_DEV)
    hot_expert = jax.random.randint(jax.random.fold_in(key, 101), (), 0, EXPERTS)
    block_keys = jax.random.split(jax.random.fold_in(key, 102), block_count)

    def one_block(block_key):
        key_order, key_count, key_slot, key_token, key_swap = jax.random.split(block_key, 5)
        ranks = jnp.arange(EXPERTS, dtype=jnp.int32)
        ordering = jax.random.permutation(key_order, EXPERTS).astype(jnp.int32)
        first_label = ordering[0]
        ordering = jnp.where(ordering == hot_expert, first_label, ordering)
        ordering = jnp.where(ranks == 0, hot_expert, ordering)
        hot_count = jax.random.randint(key_count, (), 1, 6)
        rest_total = 2 * TOK_DEV - hot_count * CAP
        others = EXPERTS - hot_count
        base_load = rest_total // others
        extra_ones = rest_total % others
        loads = jnp.where(ranks < hot_count, CAP, base_load + (ranks - hot_count < extra_ones).astype(jnp.int32))
        run_ends = jnp.cumsum(loads)
        starts = run_ends - loads
        position = jnp.arange(2 * TOK_DEV, dtype=jnp.int32)
        run_index = jnp.sum((position[:, None] >= run_ends[None, :]).astype(jnp.int32), axis=1)
        within = position - starts[run_index]
        labels = ordering[run_index]
        slot_scores = jax.random.randint(key_slot, (EXPERTS, CAP), 0, 1 << 20) * CAP + jnp.arange(CAP, dtype=jnp.int32)[None, :]
        slot_orders = jnp.argsort(slot_scores, axis=1, stable=True).astype(jnp.int32)
        slot_of = slot_orders[labels, within]
        pair_labels = jnp.stack([labels[:TOK_DEV], labels[TOK_DEV:]], axis=1)
        pair_slots = jnp.stack([slot_of[:TOK_DEV], slot_of[TOK_DEV:]], axis=1)
        swapped = jax.random.randint(key_swap, (TOK_DEV, 1), 0, 2) == 1
        pair_labels = jnp.where(swapped, pair_labels[:, ::-1], pair_labels)
        pair_slots = jnp.where(swapped, pair_slots[:, ::-1], pair_slots)
        token_order = jax.random.permutation(key_token, TOK_DEV)
        return (pair_labels[token_order], pair_slots[token_order])
    labels_all, slots_all = jax.vmap(one_block)(block_keys)
    return (labels_all.reshape(WINDOWS, WIN_TOK, 2).astype(jnp.int32), slots_all.reshape(WINDOWS, WIN_TOK, 2).astype(jnp.int32))


def draw_route_experts(key, part):
    shared = route_tables(key)
    return shared[0]


def draw_route_slots(key, part):
    shared = route_tables(key)
    return shared[1]


def draw_latent(key, part):
    key = jax.random.fold_in(key, 1)
    key_base, key_rows, key_cols = jax.random.split(key, 3)
    base_draw = jnp.clip(jax.random.normal(key_base, (WINDOWS, WIN_TOK, D), jnp.float32), -4.0, 4.0)
    row_scale = jnp.exp(jax.random.uniform(key_rows, (WINDOWS, WIN_TOK, 1), jnp.float32, math.log(0.3), math.log(3.0)))
    column_scale = jnp.exp(jax.random.uniform(key_cols, (1, 1, D), jnp.float32, math.log(0.3), math.log(3.0)))
    return (base_draw * row_scale * column_scale).astype(jnp.bfloat16)


def draw_attention_in(key, part):
    key = jax.random.fold_in(key, 2)
    key_base = jax.random.fold_in(key, 0)
    drawn = jnp.clip(jax.random.normal(key_base, (WINDOWS, WIN_TOK, 3, D), jnp.float32), -4.0, 4.0)
    return drawn.astype(jnp.bfloat16)


def shard_levels(stream_key, extent, cuts, low, high):
    def one(dim, blocks):
        steps = jax.random.uniform(jax.random.fold_in(jax.random.fold_in(stream_key, 6), dim), (blocks,), jnp.float32, low / len(cuts), high / len(cuts))
        return jnp.repeat(jnp.exp(steps), extent[dim] // blocks).reshape((-1,) + (1,) * (len(extent) - dim - 1))

    gain = one(*cuts[0])
    for cut in cuts[1:]:
        gain = gain * one(*cut)
    return gain


def gaussian(stream_key, dims, deviation, reach, cuts=(), held_as=jnp.bfloat16):
    entries = deviation * jax.random.normal(stream_key, dims, jnp.float32)
    if cuts:
        entries = entries * shard_levels(stream_key, dims, cuts, -0.22, 0.18)
    return jnp.clip(entries, -reach, reach).astype(held_as)


def setup_inputs(seed: int = 0) -> dict:
    keys = jax.random.split(jax.random.key(seed), 11)
    return {
        "latent": draw_latent(jax.random.fold_in(keys[10], 71), 0),
        "attention_in": draw_attention_in(jax.random.fold_in(keys[10], 71), 0),
        "out_weight": gaussian(keys[2], (D, D), D ** -0.5, 0.09375, ((0, 8),)),
        "modulation": gaussian(keys[3], (4, D), 1.0, 4.0, (), jnp.float32),
        "route_experts": draw_route_experts(jax.random.fold_in(keys[10], 71), 0),
        "route_slots": draw_route_slots(jax.random.fold_in(keys[10], 71), 0),
        "route_gates": jnp.clip(0.1 + 0.9 * jax.random.uniform(keys[6], (WINDOWS, WIN_TOK, 2), jnp.float32) ** shard_levels(keys[6], (WINDOWS, WIN_TOK, 2), ((0, 16), (1, 8)), -0.2, 0.2), 0.1, 1.0),
        "gate_weight": gaussian(keys[7], (EXPERTS // 2, D, 2 * FF), D ** -0.5, 0.09375, ((0, 16), (2, 8))),
        "up_weight": gaussian(keys[8], (EXPERTS // 2, D, 2 * FF), D ** -0.5, 0.09375, ((0, 16), (2, 8))),
        "down_weight": gaussian(keys[9], (EXPERTS // 2, 2 * FF, D), FF ** -0.5, 0.125, ((0, 16), (1, 8))),
    }


def reference(latent, attention_in, out_weight, modulation, route_experts, route_slots, route_gates, gate_weight, up_weight, down_weight):
    score_scale = 1.0 / math.sqrt(HD)
    group_width = GROUP_HEADS * HD

    def window(window_in):
        totals = jnp.zeros((WIN_TOK, D), jnp.float32)
        for head_group in range(N_SP):
            first = head_group * group_width
            queries = window_in[:, 0, first:first + group_width].reshape(WIN_TOK, GROUP_HEADS, HD).astype(jnp.float32)
            key_rows = window_in[:, 1, first:first + group_width].reshape(WIN_TOK, GROUP_HEADS, HD).astype(jnp.float32)
            value_rows = window_in[:, 2, first:first + group_width].reshape(WIN_TOK, GROUP_HEADS, HD).astype(jnp.float32)
            scores = jnp.einsum('qhd,khd->hqk', queries, key_rows) * score_scale
            weights = jax.nn.softmax(scores, axis=-1).astype(jnp.bfloat16)
            attended = jnp.einsum('hqk,khd->qhd', weights.astype(jnp.float32), value_rows).astype(jnp.bfloat16)
            attended = attended.reshape(WIN_TOK, group_width)
            term = jnp.dot(attended, out_weight[first:first + group_width], preferred_element_type=jnp.float32).astype(jnp.bfloat16)
            totals = totals + term.astype(jnp.float32)
        return totals
    projected = lax.map(window, attention_in)
    residual = latent.astype(jnp.float32) + modulation[0] * projected
    row_mean = lax.optimization_barrier(jnp.mean(residual, axis=-1, keepdims=True))
    centered = residual - row_mean
    variance = lax.optimization_barrier(jnp.mean(centered * centered, axis=-1, keepdims=True))
    normed = centered * lax.rsqrt(variance + 1e-06)
    moe_in = (normed * (1.0 + modulation[2]) + modulation[1]).astype(jnp.bfloat16)
    token_count = WINDOWS * WIN_TOK
    blocks = token_count // TOK_DEV
    flat_in = moe_in.reshape(token_count, D)
    padded = jnp.concatenate([flat_in, jnp.zeros((1, D), jnp.bfloat16)], axis=0)
    expert_ids = route_experts.reshape(token_count, 2).astype(jnp.int32)
    slot_ids = route_slots.reshape(token_count, 2).astype(jnp.int32)
    gate_values = route_gates.reshape(token_count, 2).astype(jnp.float32)
    token_index = jnp.broadcast_to(jnp.arange(token_count, dtype=jnp.int32)[:, None], (token_count, 2))
    block_index = token_index // TOK_DEV
    cell_index = ((expert_ids * blocks + block_index) * CAP + slot_ids).reshape(-1)
    row_table = jnp.full((EXPERTS * blocks * CAP,), token_count, jnp.int32).at[cell_index].set(token_index.reshape(-1))
    row_table = row_table.reshape(EXPERTS, blocks * CAP)
    gate_table = jnp.zeros((EXPERTS * blocks * CAP,), jnp.float32).at[cell_index].set(gate_values.reshape(-1))
    gate_table = gate_table.reshape(EXPERTS, blocks * CAP)

    def expert_step(combined, inputs):
        expert, row_index, gate_column = inputs
        rows = padded[row_index]
        pair_index = expert // 2
        half_index = expert % 2
        pair_gate = lax.dynamic_index_in_dim(gate_weight, pair_index, 0, keepdims=False)
        pair_up = lax.dynamic_index_in_dim(up_weight, pair_index, 0, keepdims=False)
        pair_down = lax.dynamic_index_in_dim(down_weight, pair_index, 0, keepdims=False)
        expert_gate = lax.dynamic_slice_in_dim(pair_gate, half_index * FF, FF, 1)
        expert_up = lax.dynamic_slice_in_dim(pair_up, half_index * FF, FF, 1)
        expert_down = lax.dynamic_slice_in_dim(pair_down, half_index * FF, FF, 0)
        output = jnp.zeros((blocks * CAP, D), jnp.float32)
        for shard_index in range(SHARDS):
            low = shard_index * SHARD_FF
            gate_part = jnp.dot(rows, expert_gate[:, low:low + SHARD_FF], preferred_element_type=jnp.float32)
            up_part = jnp.dot(rows, expert_up[:, low:low + SHARD_FF], preferred_element_type=jnp.float32)
            activation = (jax.nn.silu(gate_part) * up_part).astype(jnp.bfloat16)
            partial_value = jnp.dot(activation, expert_down[low:low + SHARD_FF], preferred_element_type=jnp.float32).astype(jnp.bfloat16)
            output = output + partial_value.astype(jnp.float32)
        combined = combined.at[row_index].add(gate_column[:, None] * output)
        return (combined, None)
    start_sum = jnp.zeros((token_count + 1, D), jnp.float32)
    combined, _ = lax.scan(expert_step, start_sum, (jnp.arange(EXPERTS, dtype=jnp.int32), row_table, gate_table))
    combined = combined[:token_count].reshape(WINDOWS, WIN_TOK, D)
    return (residual + modulation[3] * combined).astype(jnp.bfloat16)
```

```python
import functools
import math

import jax
import jax.numpy as jnp
from jax import lax
from jax.experimental import pallas as pl
from jax.experimental.pallas import tpu as pltpu
from jax.sharding import PartitionSpec as P

HD = 128
MESH = pl.DeviceIdType.MESH

PLANE = (
    (1, 0), (0, 1), (3, 0), (0, 3), (1, 1), (3, 3), (2, 0), (0, 2),
    (1, 3), (3, 1), (2, 1), (1, 2), (2, 3), (3, 2), (2, 2),
)
LINE = (1, 3, 2)
CAP = 12
BLOCK_SLOTS = 4 * CAP
LAG = 2
W_SLOTS = 3


def attend(block):
    queries = block[:, 0, 0]
    key_rows = block[:, 1, 0]
    value_rows = block[:, 2, 0]
    score_scale = 1.0 / math.sqrt(HD)
    scores = (
        jnp.einsum("qhd,khd->hqk", queries, key_rows, preferred_element_type=jnp.float32)
        * score_scale
    )
    top_rows = jnp.max(scores, axis=-1, keepdims=True)
    lifted = jnp.exp(scores - top_rows)
    weights = (lifted / jnp.sum(lifted, axis=-1, keepdims=True)).astype(jnp.bfloat16)
    mixed = jnp.einsum("hqk,khd->qhd", weights, value_rows, preferred_element_type=jnp.float32)
    return mixed.astype(jnp.bfloat16)


def expert_kernel(
    chunks,
    moe_ref, res_ref, gate_ref, packs_ref, wg_own, wg_far, wu_own, wu_far, wd_own, wd_far,
    out_ref,
    tok, send, recv, back, sums, acc_g, acc_u, act, wg, wu, wd, spread, merge, own,
    ag_s, ag_r, d_s, d_r, r_s, r_r, x_s, x_r, w_sem, wd_sem,
):
    sp, ep = lax.axis_index("sp"), lax.axis_index("ep")
    x, core = sp // 2, sp % 2
    z, y = ep // 4, ep % 4
    F = tok.shape[3]
    half = wg_own.shape[1]
    n_rows = send.shape[1]
    n_tok = 4 * tok.shape[2]
    tile = 256

    def x_peer(d):
        return (x + d) % 4

    def x_dev(d):
        return (x_peer(d) * 2 + core, ep)

    def plane_peer(o):
        return ((z + o[0]) % 4) * 4 + (y + o[1]) % 4

    barrier = pltpu.get_barrier_semaphore()
    for d in LINE:
        pl.semaphore_signal(barrier, inc=1, device_id=x_dev(d), device_id_type=MESH)
    for o in PLANE:
        pl.semaphore_signal(barrier, inc=1, device_id=(sp, plane_peer(o)), device_id_type=MESH)

    def cols(c):
        return pl.ds(pl.multiple_of(c * F, F), F)

    def seat(p):
        return pl.ds(pl.multiple_of(p * BLOCK_SLOTS, 16), BLOCK_SLOTS)

    def w_copies(k):
        s = k % W_SLOTS
        out = []
        for i, (src, dst, at) in enumerate(
            ((wg_own, wg, 0), (wg_far, wg, half), (wu_own, wu, 0), (wu_far, wu, half))
        ):
            out.append(
                pltpu.make_async_copy(src.at[cols(k), :], dst.at[s, :, pl.ds(at, half)], w_sem.at[s, i])
            )
        return out

    def wd_copies(k):
        s = k % W_SLOTS
        return [
            pltpu.make_async_copy(src.at[:, cols(k)], wd.at[s, pl.ds(at, half), :], wd_sem.at[s, i])
            for i, (src, at) in enumerate(((wd_own, 0), (wd_far, half)))
        ]

    def ag_copy(c, i):
        return pltpu.make_async_remote_copy(
            moe_ref.at[:, cols(c)], tok.at[c, x], ag_s.at[c, i], ag_r.at[c, i],
            device_id=x_dev(LINE[i]), device_id_type=MESH,
        )

    def plane_copy(c, i, dst, s_sem, r_sem):
        peer = plane_peer(PLANE[i])
        return pltpu.make_async_remote_copy(
            send.at[c, seat(peer)], dst.at[c, seat(ep)], s_sem.at[c, i], r_sem.at[c, i],
            device_id=(sp, peer), device_id_type=MESH,
        )

    def sum_copy(c, i):
        return pltpu.make_async_remote_copy(
            tok.at[c, x_peer(LINE[i])], sums.at[c, i], x_s.at[c, i], x_r.at[c, i],
            device_id=x_dev(LINE[i]), device_id_type=MESH,
        )

    for k in range(W_SLOTS):
        for cp in w_copies(k) + wd_copies(k):
            cp.start()

    pl.semaphore_wait(barrier, len(LINE) + len(PLANE))

    @pl.loop(0, chunks)
    def _(c):
        for i in range(3):
            ag_copy(c, i).start()

    row = lax.broadcasted_iota(jnp.int32, (n_rows, 1), 0)
    pair, rest = row // BLOCK_SLOTS, row % BLOCK_SLOTS
    block, slot = rest // CAP, rest % CAP
    wanted = (2 * pair + x // 2) * CAP + slot
    for b in range(4):
        at = slice(b * 128, (b + 1) * 128)
        key = jnp.where(block == b, wanted, -1).astype(jnp.float32)
        first = packs_ref[b, 0:1, :] == key
        second = packs_ref[b, 1:2, :] == key
        spread[:, at] = jnp.where(first | second, 1.0, 0.0).astype(jnp.bfloat16)
        weight = jnp.where(first, packs_ref[b, 2:3, :], 0.0) + jnp.where(second, packs_ref[b, 3:4, :], 0.0)
        merge[at, :] = weight.T.astype(jnp.bfloat16)

    acc_g[...] = jnp.zeros_like(acc_g)
    acc_u[...] = jnp.zeros_like(acc_u)

    @pl.loop(0, chunks + LAG)
    def _(step):
        @pl.when(step < chunks)
        def _():
            c = step
            tok[c, x] = moe_ref[:, cols(c)]
            for i in range(3):
                ag_copy(c, i).wait_recv()
            lines = tok[c].reshape(n_tok, F)

            @pl.loop(0, n_rows // tile)
            def _(m):
                at = pl.ds(pl.multiple_of(m * tile, tile), tile)
                send[c, at, :] = jnp.dot(
                    spread[at, :], lines, preferred_element_type=jnp.float32
                ).astype(jnp.bfloat16)

            for i in range(len(PLANE)):
                plane_copy(c, i, recv, d_s, d_r).start()
            recv[c, seat(ep), :] = send[c, seat(ep), :]

        @pl.when(step >= LAG)
        def _():
            k = step - LAG
            s = k % W_SLOTS
            for cp in w_copies(k):
                cp.wait()
            for i in range(len(PLANE)):
                plane_copy(k, i, recv, d_s, d_r).wait_recv()

            @pl.loop(0, n_rows // tile)
            def _(m):
                at = pl.ds(pl.multiple_of(m * tile, tile), tile)
                lines = recv[k, at, :]
                acc_g[at, :] += jnp.dot(lines, wg[s], preferred_element_type=jnp.float32)
                acc_u[at, :] += jnp.dot(lines, wu[s], preferred_element_type=jnp.float32)

            @pl.when(k + W_SLOTS < chunks)
            def _():
                for cp in w_copies(k + W_SLOTS):
                    cp.start()

    @pl.loop(0, n_rows // 64)
    def _(m):
        at = pl.ds(pl.multiple_of(m * 64, 64), 64)
        g = acc_g[at, :]
        act[at, :] = (g / (1.0 + jnp.exp(-g)) * acc_u[at, :]).astype(jnp.bfloat16)

    @pl.loop(0, chunks + 2 * LAG)
    def _(step):
        @pl.when(step < chunks)
        def _():
            c = step
            s = c % W_SLOTS
            for cp in wd_copies(c):
                cp.wait()
            for i in range(len(PLANE)):
                plane_copy(c, i, recv, d_s, d_r).wait_send()

            @pl.loop(0, n_rows // tile)
            def _(m):
                at = pl.ds(pl.multiple_of(m * tile, tile), tile)
                send[c, at, :] = jnp.dot(
                    act[at, :], wd[s], preferred_element_type=jnp.float32
                ).astype(jnp.bfloat16)

            for i in range(len(PLANE)):
                plane_copy(c, i, back, r_s, r_r).start()
            back[c, seat(ep), :] = send[c, seat(ep), :]

            @pl.when(c + W_SLOTS < chunks)
            def _():
                for cp in wd_copies(c + W_SLOTS):
                    cp.start()

        @pl.when((step >= LAG) & (step < chunks + LAG))
        def _():
            k = step - LAG
            for i in range(len(PLANE)):
                plane_copy(k, i, back, r_s, r_r).wait_recv()
            lines = back[k]

            @pl.loop(0, 4)
            def _(b):
                at = pl.ds(pl.multiple_of(b * 128, 128), 128)
                part = jnp.dot(merge[at, :], lines, preferred_element_type=jnp.float32)
                tok[k, b] = part.astype(jnp.bfloat16)

                @pl.when(b == x)
                def _():
                    own[k] = part

            for i in range(3):
                sum_copy(k, i).start()

        @pl.when(step >= 2 * LAG)
        def _():
            k = step - 2 * LAG
            total = own[k]
            for i in range(3):
                sum_copy(k, i).wait_recv()
                total = total + sums[k, i].astype(jnp.float32)
            out_ref[:, cols(k)] = (res_ref[:, cols(k)] + gate_ref[:, cols(k)] * total).astype(out_ref.dtype)

    @pl.loop(0, chunks)
    def _(c):
        for i in range(3):
            ag_copy(c, i).wait_send()
            sum_copy(c, i).wait_send()
        for i in range(len(PLANE)):
            plane_copy(c, i, back, r_s, r_r).wait_send()


def experts(moe_in, residual, gate_row, packs, weights):
    tokens, width = moe_in.shape
    n_ep = 16
    chunks = 8
    F = width // chunks
    rows = n_ep * BLOCK_SLOTS
    hidden = 2 * weights[0].shape[1]
    bf, f32 = jnp.bfloat16, jnp.float32
    n_plane = len(PLANE)
    dma = pltpu.SemaphoreType.DMA
    vmem = pl.BlockSpec(memory_space=pltpu.VMEM)
    hbm = pl.BlockSpec(memory_space=pl.ANY)
    return pl.pallas_call(
        functools.partial(expert_kernel, chunks),
        out_shape=jax.ShapeDtypeStruct((tokens, width), bf),
        in_specs=[vmem] * 4 + [hbm] * 6,
        out_specs=vmem,
        scratch_shapes=[
            pltpu.VMEM((chunks, 4, tokens, F), bf),
            pltpu.VMEM((chunks, rows, F), bf),
            pltpu.VMEM((chunks, rows, F), bf),
            pltpu.VMEM((chunks, rows, F), bf),
            pltpu.VMEM((chunks, 3, tokens, F), bf),
            pltpu.VMEM((rows, hidden), f32),
            pltpu.VMEM((rows, hidden), f32),
            pltpu.VMEM((rows, hidden), bf),
            pltpu.VMEM((W_SLOTS, F, hidden), bf),
            pltpu.VMEM((W_SLOTS, F, hidden), bf),
            pltpu.VMEM((W_SLOTS, hidden, F), bf),
            pltpu.VMEM((rows, 4 * tokens), bf),
            pltpu.VMEM((4 * tokens, rows), bf),
            pltpu.VMEM((chunks, tokens, F), f32),
            dma((chunks, 3)), dma((chunks, 3)),
            dma((chunks, n_plane)), dma((chunks, n_plane)),
            dma((chunks, n_plane)), dma((chunks, n_plane)),
            dma((chunks, 3)), dma((chunks, 3)),
            dma((W_SLOTS, 4)), dma((W_SLOTS, 2)),
        ],
        compiler_params=pltpu.CompilerParams(
            collective_id=0, has_side_effects=True, vmem_limit_bytes=62 * 1024 * 1024
        ),
        cost_estimate=pl.CostEstimate(flops=26_000_000_000, bytes_accessed=40_000_000, transcendentals=800_000),
        name="experts",
    )(moe_in, residual, gate_row, packs, *weights)


def local(
    latent,
    attention_in,
    out_weight,
    modulation,
    route_experts,
    route_slots,
    route_gates,
    gate_weight,
    up_weight,
    down_weight,
):
    n_sp = lax.axis_size("sp")
    tokens = latent.shape[1]
    group_heads = out_weight.shape[0] // HD
    window_len = tokens * n_sp
    core = lax.axis_index("sp") % 2

    swap = [(i, i ^ 1) for i in range(n_sp)]
    weights = []
    for w in (gate_weight[0], up_weight[0], down_weight[0]):
        weights += [w, lax.ppermute(w, "sp", swap)]

    cells = (route_experts[0] * CAP + route_slots[0]).astype(jnp.float32)
    pack = jnp.concatenate([cells, route_gates[0], jnp.zeros((tokens, 4), jnp.float32)], axis=1).T
    packs = lax.all_gather(pack, "sp").reshape(n_sp // 2, 2, 8, tokens)
    packs = lax.dynamic_index_in_dim(packs, core, 1, keepdims=False)

    packed = attention_in[0].reshape(tokens, 3, n_sp, group_heads, HD)
    attended = attend(lax.all_to_all(packed, "sp", split_axis=2, concat_axis=0, tiled=True))
    flat_heads = attended.reshape(window_len, group_heads * HD)
    projected = lax.psum_scatter(
        jnp.dot(flat_heads, out_weight, preferred_element_type=jnp.float32).astype(jnp.bfloat16),
        "sp",
        scatter_dimension=0,
        tiled=True,
    ).astype(jnp.float32)
    residual = latent[0].astype(jnp.float32) + modulation[0] * projected
    row_mean = jnp.mean(residual, axis=-1, keepdims=True)
    centered = residual - row_mean
    variance = jnp.mean(centered * centered, axis=-1, keepdims=True)
    normed = centered * lax.rsqrt(variance + 1e-06)
    moe_in = (normed * (1.0 + modulation[2]) + modulation[1]).astype(jnp.bfloat16)
    return experts(moe_in, residual, modulation[3:4], packs, weights)[None]


def solution(mesh):
    return jax.shard_map(
        local,
        mesh=mesh,
        in_specs=(
            P("ep", "sp", None),
            P("ep", "sp", None, None),
            P("sp", None),
            P(),
            P("ep", "sp", None),
            P("ep", "sp", None),
            P("ep", "sp", None),
            P("ep", None, "sp"),
            P("ep", None, "sp"),
            P("ep", "sp", None),
        ),
        out_specs=P("ep", "sp", None),
        check_vma=False,
    )
```

```python
import functools
import math

import jax
import jax.numpy as jnp
from jax import lax
from jax.experimental import pallas as pl
from jax.experimental.pallas import tpu as pltpu
from jax.sharding import PartitionSpec as P

HD = 128
MESH = pl.DeviceIdType.MESH

PLANE = (
    (1, 0), (0, 1), (3, 0), (0, 3), (1, 1), (3, 3), (2, 0), (0, 2),
    (1, 3), (3, 1), (2, 1), (1, 2), (2, 3), (3, 2), (2, 2),
)
LINE = (1, 3, 2)
CAP = 12
BLOCK_SLOTS = 4 * CAP
LAG = 2
W_SLOTS = 3


def attention_kernel(
    chunks,
    qkv_ref, latent_ref, wo_ref, mod_ref, pack_ref, wg_ref, wu_ref, wd_ref,
    moe_ref, res_ref, packs_ref, wg_far, wu_far, wd_far,
    heads, values, att, pair_out, pair_in, turn_out, turn_in, side, side_out, side_in, own,
    q_s, q_r, q_l, p_s, p_r, t_s, t_r, s_s, s_r, w_s, w_r, k_s, k_r, k_l,
):
    sp, ep = lax.axis_index("sp"), lax.axis_index("ep")
    x, core = sp // 2, sp % 2
    n_heads, _, window, hd = heads.shape
    tokens = window // 8
    F = wo_ref.shape[1] // chunks
    H = F // 2
    f32, bf = jnp.float32, jnp.bfloat16

    def x_peer(d):
        return (x + d) % 4

    def x_dev(d):
        return (x_peer(d) * 2 + core, ep)

    partner = (x * 2 + 1 - core, ep)
    others = [(d, k) for d in (2, 1, 3, 0) for k in (0, 1) if (d, k) != (0, 0)]

    def other(i):
        d, k = others[i]
        return x_peer(d) * 2 + (core + k) % 2

    def cols(c):
        return pl.ds(pl.multiple_of(c * F, F), F)

    def block(s):
        return pl.ds(pl.multiple_of(s * tokens, tokens), tokens)

    def head_cols(s, h):
        return pl.ds(pl.multiple_of((s * n_heads + h) * hd, hd), hd)

    def head_copy(h, i):
        to = other(i)
        return pltpu.make_async_remote_copy(
            qkv_ref.at[:, :, head_cols(to, h)], heads.at[h, :, block(sp), :], q_s.at[h, i], q_r.at[h, i],
            device_id=(to, ep), device_id_type=MESH,
        )

    def head_local(h):
        return pltpu.make_async_copy(
            qkv_ref.at[:, :, head_cols(sp, h)], heads.at[h, :, block(sp), :], q_l.at[h]
        )

    def weight_copy(i):
        src, dst = ((wg_ref, wg_far), (wu_ref, wu_far), (wd_ref, wd_far))[i]
        return pltpu.make_async_remote_copy(
            src, dst, w_s.at[i], w_r.at[i], device_id=partner, device_id_type=MESH
        )

    def pack_copy(i):
        return pltpu.make_async_remote_copy(
            pack_ref, packs_ref.at[x], k_s.at[i], k_r.at[i], device_id=x_dev(LINE[i]), device_id_type=MESH
        )

    pack_local = pltpu.make_async_copy(pack_ref, packs_ref.at[x], k_l)

    def pair_copy(c):
        return pltpu.make_async_remote_copy(
            pair_out.at[c], pair_in.at[c], p_s.at[c], p_r.at[c], device_id=partner, device_id_type=MESH
        )

    def turn_copy(c, i):
        return pltpu.make_async_remote_copy(
            turn_out.at[c, i], turn_in.at[c, i], t_s.at[c, i], t_r.at[c, i],
            device_id=x_dev((3, 1)[i]), device_id_type=MESH,
        )

    def side_copy(c, i):
        return pltpu.make_async_remote_copy(
            side_out.at[c, i], side_in.at[c, i], s_s.at[c, i], s_r.at[c, i],
            device_id=x_dev((3, 1)[i]), device_id_type=MESH,
        )

    barrier = pltpu.get_barrier_semaphore()
    for i in range(7):
        pl.semaphore_signal(barrier, inc=1, device_id=(other(i), ep), device_id_type=MESH)
    pack_local.start()
    for h in range(n_heads):
        head_local(h).start()
    pl.semaphore_wait(barrier, 7)

    @pl.loop(0, n_heads)
    def _(h):
        for i in range(7):
            head_copy(h, i).start()

    for i in range(3):
        pack_copy(i).start()
    for i in range(3):
        weight_copy(i).start()

    values[:, hd:] = jnp.ones((window, hd), bf)
    factor = math.log2(math.e) / math.sqrt(hd)
    q_tile = 2 * tokens

    @pl.loop(0, n_heads)
    def _(h):
        head_local(h).wait()
        for i in range(7):
            head_copy(h, i).wait_recv()
        values[:, :hd] = heads[h, 2]

        @pl.loop(0, window // q_tile)
        def _(m):
            at = pl.ds(pl.multiple_of(m * q_tile, q_tile), q_tile)
            scores = lax.dot_general(
                heads[h, 0, at, :], heads[h, 1], (((1,), (1,)), ((), ())), preferred_element_type=f32
            )
            top = jnp.max(scores, axis=1, keepdims=True)
            lifted = jnp.exp2((scores - top) * factor).astype(bf)
            mixed = jnp.dot(lifted, values[...], preferred_element_type=f32)
            out = (mixed[:, :hd] / mixed[:, hd:]).astype(bf)
            to = (block(m), pl.ds(pl.multiple_of(h * hd, hd), hd))
            att[0, to[0], to[1]] = out[:tokens]
            att[1, to[0], to[1]] = out[tokens:]

    @pl.loop(0, chunks + 4)
    def _(step):
        @pl.when(step < chunks)
        def _():
            c = step
            far = jnp.dot(att[1 - core], wo_ref[:, cols(c)], preferred_element_type=f32)
            pair_out[c] = far.astype(bf)
            pair_copy(c).start()

        @pl.when((step >= 1) & (step < chunks + 1))
        def _():
            c = step - 1
            pair_copy(c).wait_recv()

            def part(b):
                return jnp.dot(
                    att[core, block(b), :], wo_ref[:, cols(c)], preferred_element_type=f32
                ) + pair_in[c, block(b), :].astype(f32)

            over = part(x_peer(2)).astype(bf)
            for i in range(2):
                turn_out[c, i] = over[:, i * H : (i + 1) * H]
                turn_copy(c, i).start()
            side[c, 0] = part(x_peer(3))
            side[c, 1] = part(x_peer(1))
            own[c] = part(x)

        @pl.when((step >= 2) & (step < chunks + 2))
        def _():
            c = step - 2
            for i in range(2):
                turn_copy(c, i).wait_recv()
                near = slice(i * H, (i + 1) * H)
                rest = slice((1 - i) * H, (2 - i) * H)
                side_out[c, i, :, near] = (side[c, i, :, near] + turn_in[c, i].astype(f32)).astype(bf)
                side_out[c, i, :, rest] = side[c, i, :, rest].astype(bf)
                side_copy(c, i).start()

        @pl.when(step >= 4)
        def _():
            c = step - 4
            total = own[c]
            for i in range(2):
                side_copy(c, i).wait_recv()
                total = total + side_in[c, i].astype(f32)
            res_ref[:, cols(c)] = latent_ref[:, cols(c)].astype(f32) + mod_ref[0:1, cols(c)] * total

    @pl.loop(0, tokens // 16)
    def _(m):
        at = pl.ds(pl.multiple_of(m * 16, 16), 16)
        rows = res_ref[at, :]
        centered = rows - jnp.mean(rows, axis=1, keepdims=True)
        variance = jnp.mean(centered * centered, axis=1, keepdims=True)
        normed = centered * lax.rsqrt(variance + 1e-06)
        moe_ref[at, :] = (normed * (1.0 + mod_ref[2:3, :]) + mod_ref[1:2, :]).astype(bf)

    pack_local.wait()
    for i in range(3):
        pack_copy(i).wait()
        weight_copy(i).wait()

    @pl.loop(0, n_heads)
    def _(h):
        for i in range(7):
            head_copy(h, i).wait_send()

    @pl.loop(0, chunks)
    def _(c):
        pair_copy(c).wait_send()
        for i in range(2):
            turn_copy(c, i).wait_send()
            side_copy(c, i).wait_send()


def attention(qkv, latent, out_weight, modulation, pack, weights):
    tokens, width = latent.shape
    chunks = 8
    F = width // chunks
    group = out_weight.shape[0]
    window = 8 * tokens
    bf, f32 = jnp.bfloat16, jnp.float32
    dma = pltpu.SemaphoreType.DMA
    vmem = pl.BlockSpec(memory_space=pltpu.VMEM)
    hbm = pl.BlockSpec(memory_space=pl.ANY)
    outs = pl.pallas_call(
        functools.partial(attention_kernel, chunks),
        out_shape=[
            jax.ShapeDtypeStruct((tokens, width), bf),
            jax.ShapeDtypeStruct((tokens, width), f32),
            jax.ShapeDtypeStruct((4,) + pack.shape, f32),
        ]
        + [jax.ShapeDtypeStruct(w.shape, bf) for w in weights],
        in_specs=[hbm] + [vmem] * 3 + [hbm] * 4,
        out_specs=[vmem] * 2 + [hbm] * 4,
        scratch_shapes=[
            pltpu.VMEM((group // HD, 3, window, HD), bf),
            pltpu.VMEM((window, 2 * HD), bf),
            pltpu.VMEM((2, window // 2, group), bf),
            pltpu.VMEM((chunks, window // 2, F), bf),
            pltpu.VMEM((chunks, window // 2, F), bf),
            pltpu.VMEM((chunks, 2, tokens, F // 2), bf),
            pltpu.VMEM((chunks, 2, tokens, F // 2), bf),
            pltpu.VMEM((chunks, 2, tokens, F), f32),
            pltpu.VMEM((chunks, 2, tokens, F), bf),
            pltpu.VMEM((chunks, 2, tokens, F), bf),
            pltpu.VMEM((chunks, tokens, F), f32),
            dma((4, 7)), dma((4, 7)), dma((4,)),
            dma((chunks,)), dma((chunks,)),
            dma((chunks, 2)), dma((chunks, 2)),
            dma((chunks, 2)), dma((chunks, 2)),
            dma((3,)), dma((3,)), dma((3,)), dma((3,)), dma,
        ],
        compiler_params=pltpu.CompilerParams(
            collective_id=1, has_side_effects=True, vmem_limit_bytes=60 * 1024 * 1024
        ),
        cost_estimate=pl.CostEstimate(flops=6_500_000_000, bytes_accessed=40_000_000, transcendentals=4_200_000),
        name="attention",
    )(qkv, latent, out_weight, modulation, pack, *weights)
    return outs[0], outs[1], outs[2], outs[3:]


def expert_kernel(
    chunks,
    moe_ref, res_ref, gate_ref, packs_ref, wg_own, wg_far, wu_own, wu_far, wd_own, wd_far,
    out_ref,
    tok, send, recv, back, sums, acc_g, acc_u, act, wg, wu, wd, spread, merge, own,
    ag_s, ag_r, d_s, d_r, r_s, r_r, x_s, x_r, w_sem, wd_sem,
):
    sp, ep = lax.axis_index("sp"), lax.axis_index("ep")
    x, core = sp // 2, sp % 2
    z, y = ep // 4, ep % 4
    F = tok.shape[3]
    half = wg_own.shape[1]
    n_rows = send.shape[1]
    n_tok = 4 * tok.shape[2]
    tile = 256

    def x_peer(d):
        return (x + d) % 4

    def x_dev(d):
        return (x_peer(d) * 2 + core, ep)

    def plane_peer(o):
        return ((z + o[0]) % 4) * 4 + (y + o[1]) % 4

    barrier = pltpu.get_barrier_semaphore()
    for d in LINE:
        pl.semaphore_signal(barrier, inc=1, device_id=x_dev(d), device_id_type=MESH)
    for o in PLANE:
        pl.semaphore_signal(barrier, inc=1, device_id=(sp, plane_peer(o)), device_id_type=MESH)

    def cols(c):
        return pl.ds(pl.multiple_of(c * F, F), F)

    def seat(p):
        return pl.ds(pl.multiple_of(p * BLOCK_SLOTS, 16), BLOCK_SLOTS)

    def w_copies(k):
        s = k % W_SLOTS
        out = []
        for i, (src, dst, at) in enumerate(
            ((wg_own, wg, 0), (wg_far, wg, half), (wu_own, wu, 0), (wu_far, wu, half))
        ):
            out.append(
                pltpu.make_async_copy(src.at[cols(k), :], dst.at[s, :, pl.ds(at, half)], w_sem.at[s, i])
            )
        return out

    def wd_copies(k):
        s = k % W_SLOTS
        return [
            pltpu.make_async_copy(src.at[:, cols(k)], wd.at[s, pl.ds(at, half), :], wd_sem.at[s, i])
            for i, (src, at) in enumerate(((wd_own, 0), (wd_far, half)))
        ]

    def ag_copy(c, i):
        return pltpu.make_async_remote_copy(
            moe_ref.at[:, cols(c)], tok.at[c, x], ag_s.at[c, i], ag_r.at[c, i],
            device_id=x_dev(LINE[i]), device_id_type=MESH,
        )

    def plane_copy(c, i, dst, s_sem, r_sem):
        peer = plane_peer(PLANE[i])
        return pltpu.make_async_remote_copy(
            send.at[c, seat(peer)], dst.at[c, seat(ep)], s_sem.at[c, i], r_sem.at[c, i],
            device_id=(sp, peer), device_id_type=MESH,
        )

    def sum_copy(c, i):
        return pltpu.make_async_remote_copy(
            tok.at[c, x_peer(LINE[i])], sums.at[c, i], x_s.at[c, i], x_r.at[c, i],
            device_id=x_dev(LINE[i]), device_id_type=MESH,
        )

    for k in range(W_SLOTS):
        for cp in w_copies(k) + wd_copies(k):
            cp.start()

    pl.semaphore_wait(barrier, len(LINE) + len(PLANE))

    @pl.loop(0, chunks)
    def _(c):
        for i in range(3):
            ag_copy(c, i).start()

    row = lax.broadcasted_iota(jnp.int32, (n_rows, 1), 0)
    pair, rest = row // BLOCK_SLOTS, row % BLOCK_SLOTS
    block, slot = rest // CAP, rest % CAP
    wanted = (2 * pair + x // 2) * CAP + slot
    for b in range(4):
        at = slice(b * 128, (b + 1) * 128)
        key = jnp.where(block == b, wanted, -1).astype(jnp.float32)
        first = packs_ref[b, 0:1, :] == key
        second = packs_ref[b, 1:2, :] == key
        spread[:, at] = jnp.where(first | second, 1.0, 0.0).astype(jnp.bfloat16)
        weight = jnp.where(first, packs_ref[b, 2:3, :], 0.0) + jnp.where(second, packs_ref[b, 3:4, :], 0.0)
        merge[at, :] = weight.T.astype(jnp.bfloat16)

    acc_g[...] = jnp.zeros_like(acc_g)
    acc_u[...] = jnp.zeros_like(acc_u)

    @pl.loop(0, chunks + LAG)
    def _(step):
        @pl.when(step < chunks)
        def _():
            c = step
            tok[c, x] = moe_ref[:, cols(c)]
            for i in range(3):
                ag_copy(c, i).wait_recv()
            lines = tok[c].reshape(n_tok, F)

            @pl.loop(0, n_rows // tile)
            def _(m):
                at = pl.ds(pl.multiple_of(m * tile, tile), tile)
                send[c, at, :] = jnp.dot(
                    spread[at, :], lines, preferred_element_type=jnp.float32
                ).astype(jnp.bfloat16)

            for i in range(len(PLANE)):
                plane_copy(c, i, recv, d_s, d_r).start()
            recv[c, seat(ep), :] = send[c, seat(ep), :]

        @pl.when(step >= LAG)
        def _():
            k = step - LAG
            s = k % W_SLOTS
            for cp in w_copies(k):
                cp.wait()
            for i in range(len(PLANE)):
                plane_copy(k, i, recv, d_s, d_r).wait_recv()

            @pl.loop(0, n_rows // tile)
            def _(m):
                at = pl.ds(pl.multiple_of(m * tile, tile), tile)
                lines = recv[k, at, :]
                acc_g[at, :] += jnp.dot(lines, wg[s], preferred_element_type=jnp.float32)
                acc_u[at, :] += jnp.dot(lines, wu[s], preferred_element_type=jnp.float32)

            @pl.when(k + W_SLOTS < chunks)
            def _():
                for cp in w_copies(k + W_SLOTS):
                    cp.start()

    @pl.loop(0, n_rows // 64)
    def _(m):
        at = pl.ds(pl.multiple_of(m * 64, 64), 64)
        g = acc_g[at, :]
        act[at, :] = (g / (1.0 + jnp.exp(-g)) * acc_u[at, :]).astype(jnp.bfloat16)

    @pl.loop(0, chunks + 2 * LAG)
    def _(step):
        @pl.when(step < chunks)
        def _():
            c = step
            s = c % W_SLOTS
            for cp in wd_copies(c):
                cp.wait()
            for i in range(len(PLANE)):
                plane_copy(c, i, recv, d_s, d_r).wait_send()

            @pl.loop(0, n_rows // tile)
            def _(m):
                at = pl.ds(pl.multiple_of(m * tile, tile), tile)
                send[c, at, :] = jnp.dot(
                    act[at, :], wd[s], preferred_element_type=jnp.float32
                ).astype(jnp.bfloat16)

            for i in range(len(PLANE)):
                plane_copy(c, i, back, r_s, r_r).start()
            back[c, seat(ep), :] = send[c, seat(ep), :]

            @pl.when(c + W_SLOTS < chunks)
            def _():
                for cp in wd_copies(c + W_SLOTS):
                    cp.start()

        @pl.when((step >= LAG) & (step < chunks + LAG))
        def _():
            k = step - LAG
            for i in range(len(PLANE)):
                plane_copy(k, i, back, r_s, r_r).wait_recv()
            lines = back[k]

            @pl.loop(0, 4)
            def _(b):
                at = pl.ds(pl.multiple_of(b * 128, 128), 128)
                part = jnp.dot(merge[at, :], lines, preferred_element_type=jnp.float32)
                tok[k, b] = part.astype(jnp.bfloat16)

                @pl.when(b == x)
                def _():
                    own[k] = part

            for i in range(3):
                sum_copy(k, i).start()

        @pl.when(step >= 2 * LAG)
        def _():
            k = step - 2 * LAG
            total = own[k]
            for i in range(3):
                sum_copy(k, i).wait_recv()
                total = total + sums[k, i].astype(jnp.float32)
            out_ref[:, cols(k)] = (res_ref[:, cols(k)] + gate_ref[:, cols(k)] * total).astype(out_ref.dtype)

    @pl.loop(0, chunks)
    def _(c):
        for i in range(3):
            ag_copy(c, i).wait_send()
            sum_copy(c, i).wait_send()
        for i in range(len(PLANE)):
            plane_copy(c, i, back, r_s, r_r).wait_send()


def experts(moe_in, residual, gate_row, packs, weights):
    tokens, width = moe_in.shape
    n_ep = 16
    chunks = 8
    F = width // chunks
    rows = n_ep * BLOCK_SLOTS
    hidden = 2 * weights[0].shape[1]
    bf, f32 = jnp.bfloat16, jnp.float32
    n_plane = len(PLANE)
    dma = pltpu.SemaphoreType.DMA
    vmem = pl.BlockSpec(memory_space=pltpu.VMEM)
    hbm = pl.BlockSpec(memory_space=pl.ANY)
    return pl.pallas_call(
        functools.partial(expert_kernel, chunks),
        out_shape=jax.ShapeDtypeStruct((tokens, width), bf),
        in_specs=[vmem] * 4 + [hbm] * 6,
        out_specs=vmem,
        scratch_shapes=[
            pltpu.VMEM((chunks, 4, tokens, F), bf),
            pltpu.VMEM((chunks, rows, F), bf),
            pltpu.VMEM((chunks, rows, F), bf),
            pltpu.VMEM((chunks, rows, F), bf),
            pltpu.VMEM((chunks, 3, tokens, F), bf),
            pltpu.VMEM((rows, hidden), f32),
            pltpu.VMEM((rows, hidden), f32),
            pltpu.VMEM((rows, hidden), bf),
            pltpu.VMEM((W_SLOTS, F, hidden), bf),
            pltpu.VMEM((W_SLOTS, F, hidden), bf),
            pltpu.VMEM((W_SLOTS, hidden, F), bf),
            pltpu.VMEM((rows, 4 * tokens), bf),
            pltpu.VMEM((4 * tokens, rows), bf),
            pltpu.VMEM((chunks, tokens, F), f32),
            dma((chunks, 3)), dma((chunks, 3)),
            dma((chunks, n_plane)), dma((chunks, n_plane)),
            dma((chunks, n_plane)), dma((chunks, n_plane)),
            dma((chunks, 3)), dma((chunks, 3)),
            dma((W_SLOTS, 4)), dma((W_SLOTS, 2)),
        ],
        compiler_params=pltpu.CompilerParams(
            collective_id=0, has_side_effects=True, vmem_limit_bytes=62 * 1024 * 1024
        ),
        cost_estimate=pl.CostEstimate(flops=26_000_000_000, bytes_accessed=40_000_000, transcendentals=800_000),
        name="experts",
    )(moe_in, residual, gate_row, packs, *weights)


def local(
    latent,
    attention_in,
    out_weight,
    modulation,
    route_experts,
    route_slots,
    route_gates,
    gate_weight,
    up_weight,
    down_weight,
):
    tokens = latent.shape[1]
    weights = [gate_weight[0], up_weight[0], down_weight[0]]
    cells = (route_experts[0] * CAP + route_slots[0]).astype(jnp.float32)
    pack = jnp.concatenate([cells, route_gates[0], jnp.zeros((tokens, 4), jnp.float32)], axis=1).T
    qkv = jnp.transpose(attention_in[0], (1, 0, 2))
    moe_in, residual, packs, far = attention(qkv, latent[0], out_weight, modulation, pack, weights)
    both = [w for pair in zip(weights, far) for w in pair]
    return experts(moe_in, residual, modulation[3:4], packs, both)[None]


def solution(mesh):
    return jax.shard_map(
        local,
        mesh=mesh,
        in_specs=(
            P("ep", "sp", None),
            P("ep", "sp", None, None),
            P("sp", None),
            P(),
            P("ep", "sp", None),
            P("ep", "sp", None),
            P("ep", "sp", None),
            P("ep", None, "sp"),
            P("ep", None, "sp"),
            P("ep", "sp", None),
        ),
        out_specs=P("ep", "sp", None),
        check_vma=False,
    )
```

```python
import functools
import math

import jax
import jax.numpy as jnp
from jax import lax
from jax.experimental import pallas as pl
from jax.experimental.pallas import tpu as pltpu
from jax.sharding import PartitionSpec as P

HD = 128
MESH = pl.DeviceIdType.MESH

PLANE = (
    (1, 0), (0, 1), (3, 0), (0, 3), (1, 1), (3, 3), (2, 0), (0, 2),
    (1, 3), (3, 1), (2, 1), (1, 2), (2, 3), (3, 2), (2, 2),
)
LINE = (1, 3, 2)
CAP = 12
BLOCK_SLOTS = 4 * CAP
FAR_LATE = 8
W_SLOTS = 3
D_SLOTS = 5
SHARED = 3
SET_ORDER = (1, 2, 4, 7, 3, 6, 5)


def attention_kernel(
    chunks,
    qkv_ref, latent_ref, wo_ref, mod_ref, experts_ref, slots_ref, gates_ref, wg_ref, wu_ref, wd_ref,
    moe_ref, res_ref, packs_ref, wg_far, wu_far, wd_far,
    pack_ref, heads, values, att, pair_out, pair_in, turn_out, turn_in, side, side_out, side_in, own,
    q_s, q_r, q_l, p_s, p_r, t_s, t_r, s_s, s_r, w_s, w_r, k_s, k_r, k_l,
):
    sp, ep = lax.axis_index("sp"), lax.axis_index("ep")
    x, core = sp // 2, sp % 2
    n_heads, _, window, hd = heads.shape
    tokens = window // 8
    F = wo_ref.shape[1] // chunks
    H = F // 2
    f32, bf = jnp.float32, jnp.bfloat16

    def x_peer(d):
        return (x + d) % 4

    def x_dev(d):
        return (x_peer(d) * 2 + core, ep)

    partner = (x * 2 + 1 - core, ep)
    others = [(d, k) for d in (2, 1, 3, 0) for k in (0, 1) if (d, k) != (0, 0)]

    def other(i):
        d, k = others[i]
        return x_peer(d) * 2 + (core + k) % 2

    def cols(c):
        return pl.ds(pl.multiple_of(c * F, F), F)

    def block(s):
        return pl.ds(pl.multiple_of(s * tokens, tokens), tokens)

    def head_cols(s, h):
        return pl.ds(pl.multiple_of((s * n_heads + h) * hd, hd), hd)

    def head_copy(h, i):
        to = other(i)
        return pltpu.make_async_remote_copy(
            qkv_ref.at[:, :, head_cols(to, h)], heads.at[h, :, block(sp), :], q_s.at[h, i], q_r.at[h, i],
            device_id=(to, ep), device_id_type=MESH,
        )

    def head_local(h):
        return pltpu.make_async_copy(
            qkv_ref.at[:, :, head_cols(sp, h)], heads.at[h, :, block(sp), :], q_l.at[h]
        )

    def weight_copy(i):
        src, dst = ((wg_ref, wg_far), (wu_ref, wu_far), (wd_ref, wd_far))[i]
        return pltpu.make_async_remote_copy(
            src, dst, w_s.at[i], w_r.at[i], device_id=partner, device_id_type=MESH
        )

    def pack_copy(i):
        return pltpu.make_async_remote_copy(
            pack_ref, packs_ref.at[x], k_s.at[i], k_r.at[i], device_id=x_dev(LINE[i]), device_id_type=MESH
        )

    pack_local = pltpu.make_async_copy(pack_ref, packs_ref.at[x], k_l)

    def pair_copy(c):
        return pltpu.make_async_remote_copy(
            pair_out.at[c], pair_in.at[c], p_s.at[c], p_r.at[c], device_id=partner, device_id_type=MESH
        )

    def turn_copy(c, i):
        return pltpu.make_async_remote_copy(
            turn_out.at[c, i], turn_in.at[c, i], t_s.at[c, i], t_r.at[c, i],
            device_id=x_dev((3, 1)[i]), device_id_type=MESH,
        )

    def side_copy(c, i):
        return pltpu.make_async_remote_copy(
            side_out.at[c, i], side_in.at[c, i], s_s.at[c, i], s_r.at[c, i],
            device_id=x_dev((3, 1)[i]), device_id_type=MESH,
        )

    barrier = pltpu.get_barrier_semaphore()
    for i in range(7):
        pl.semaphore_signal(barrier, inc=1, device_id=(other(i), ep), device_id_type=MESH)
    for h in range(n_heads):
        head_local(h).start()
    pack_ref[0:2, :] = (experts_ref[...] * CAP + slots_ref[...]).astype(f32)
    pack_ref[2:4, :] = gates_ref[...]
    pack_ref[4:8, :] = jnp.zeros((4, tokens), f32)
    pack_local.start()
    pl.semaphore_wait(barrier, 7)

    @pl.loop(0, n_heads)
    def _(h):
        for i in range(7):
            head_copy(h, i).start()

    for i in range(3):
        pack_copy(i).start()
    for i in range(3):
        weight_copy(i).start()

    values[:, hd:] = jnp.ones((window, hd), bf)
    factor = math.log2(math.e) / math.sqrt(hd)
    q_tile = 2 * tokens

    @pl.loop(0, n_heads)
    def _(h):
        head_local(h).wait()
        for i in range(7):
            head_copy(h, i).wait_recv()
        values[:, :hd] = heads[h, 2]

        @pl.loop(0, window // q_tile)
        def _(m):
            at = pl.ds(pl.multiple_of(m * q_tile, q_tile), q_tile)
            scores = lax.dot_general(
                heads[h, 0, at, :], heads[h, 1], (((1,), (1,)), ((), ())), preferred_element_type=f32
            )
            top = jnp.max(scores, axis=1, keepdims=True)
            lifted = jnp.exp2((scores - top) * factor).astype(bf)
            mixed = jnp.dot(lifted, values[...], preferred_element_type=f32)
            out = (mixed[:, :hd] / mixed[:, hd:]).astype(bf)
            to = (block(m), pl.ds(pl.multiple_of(h * hd, hd), hd))
            att[0, to[0], to[1]] = out[:tokens]
            att[1, to[0], to[1]] = out[tokens:]

    far_at = (1 - core) * FAR_LATE
    sum_at = 1 + core * (chunks - 1)

    @pl.loop(0, 2 * chunks + 5)
    def _(step):
        @pl.when((step >= far_at) & (step < far_at + chunks))
        def _():
            c = step - far_at
            far = jnp.dot(att[1 - core], wo_ref[:, cols(c)], preferred_element_type=f32)
            pair_out[c] = far.astype(bf)
            pair_copy(c).start()

        @pl.when((step >= sum_at) & (step < sum_at + chunks))
        def _():
            c = step - sum_at
            pair_copy(c).wait_recv()

            def part(b):
                return jnp.dot(
                    att[core, block(b), :], wo_ref[:, cols(c)], preferred_element_type=f32
                ) + pair_in[c, block(b), :].astype(f32)

            over = part(x_peer(2)).astype(bf)
            for i in range(2):
                turn_out[c, i] = over[:, i * H : (i + 1) * H]
                turn_copy(c, i).start()
            side[c, 0] = part(x_peer(3))
            side[c, 1] = part(x_peer(1))
            own[c] = part(x)

        @pl.when((step >= sum_at + 2) & (step < sum_at + chunks + 2))
        def _():
            c = step - sum_at - 2
            for i in range(2):
                turn_copy(c, i).wait_recv()
                near = slice(i * H, (i + 1) * H)
                rest = slice((1 - i) * H, (2 - i) * H)
                side_out[c, i, :, near] = (side[c, i, :, near] + turn_in[c, i].astype(f32)).astype(bf)
                side_out[c, i, :, rest] = side[c, i, :, rest].astype(bf)
                side_copy(c, i).start()

        @pl.when((step >= sum_at + 5) & (step < sum_at + chunks + 5))
        def _():
            c = step - sum_at - 5
            total = own[c]
            for i in range(2):
                side_copy(c, i).wait_recv()
                total = total + side_in[c, i].astype(f32)
            res_ref[:, cols(c)] = latent_ref[:, cols(c)].astype(f32) + mod_ref[0:1, cols(c)] * total

    @pl.loop(0, tokens // 16)
    def _(m):
        at = pl.ds(pl.multiple_of(m * 16, 16), 16)
        rows = res_ref[at, :]
        centered = rows - jnp.mean(rows, axis=1, keepdims=True)
        variance = jnp.mean(centered * centered, axis=1, keepdims=True)
        normed = centered * lax.rsqrt(variance + 1e-06)
        moe_ref[at, :] = (normed * (1.0 + mod_ref[2:3, :]) + mod_ref[1:2, :]).astype(bf)

    pack_local.wait()
    for i in range(3):
        pack_copy(i).wait()
        weight_copy(i).wait()

    @pl.loop(0, n_heads)
    def _(h):
        for i in range(7):
            head_copy(h, i).wait_send()

    @pl.loop(0, chunks)
    def _(c):
        pair_copy(c).wait_send()
        for i in range(2):
            turn_copy(c, i).wait_send()
            side_copy(c, i).wait_send()


def attention(qkv, latent, out_weight, modulation, routes, weights):
    tokens, width = latent.shape
    chunks = 8
    F = width // chunks
    group = out_weight.shape[0]
    window = 8 * tokens
    bf, f32 = jnp.bfloat16, jnp.float32
    dma = pltpu.SemaphoreType.DMA
    vmem = pl.BlockSpec(memory_space=pltpu.VMEM)
    hbm = pl.BlockSpec(memory_space=pl.ANY)
    outs = pl.pallas_call(
        functools.partial(attention_kernel, chunks),
        out_shape=[
            jax.ShapeDtypeStruct((tokens, width), bf),
            jax.ShapeDtypeStruct((tokens, width), f32),
            jax.ShapeDtypeStruct((4, 8, tokens), f32),
        ]
        + [jax.ShapeDtypeStruct(w.shape, bf) for w in weights],
        in_specs=[hbm] + [vmem] * 6 + [hbm] * 3,
        out_specs=[vmem] * 2 + [hbm] * 4,
        scratch_shapes=[
            pltpu.VMEM((8, tokens), f32),
            pltpu.VMEM((group // HD, 3, window, HD), bf),
            pltpu.VMEM((window, 2 * HD), bf),
            pltpu.VMEM((2, window // 2, group), bf),
            pltpu.VMEM((chunks, window // 2, F), bf),
            pltpu.VMEM((chunks, window // 2, F), bf),
            pltpu.VMEM((chunks, 2, tokens, F // 2), bf),
            pltpu.VMEM((chunks, 2, tokens, F // 2), bf),
            pltpu.VMEM((chunks, 2, tokens, F), f32),
            pltpu.VMEM((chunks, 2, tokens, F), bf),
            pltpu.VMEM((chunks, 2, tokens, F), bf),
            pltpu.VMEM((chunks, tokens, F), f32),
            dma((4, 7)), dma((4, 7)), dma((4,)),
            dma((chunks,)), dma((chunks,)),
            dma((chunks, 2)), dma((chunks, 2)),
            dma((chunks, 2)), dma((chunks, 2)),
            dma((3,)), dma((3,)), dma((3,)), dma((3,)), dma,
        ],
        compiler_params=pltpu.CompilerParams(
            collective_id=1, has_side_effects=True, vmem_limit_bytes=60 * 1024 * 1024
        ),
        cost_estimate=pl.CostEstimate(flops=6_500_000_000, bytes_accessed=40_000_000, transcendentals=4_200_000),
        name="attention",
    )(qkv, latent, out_weight, modulation, *routes, *weights)
    return outs[0], outs[1], outs[2], outs[3:]


def expert_kernel(
    chunks,
    moe_ref, res_ref, mod_ref, packs_ref, wg_own, wg_far, wu_own, wu_far, wd_own, wd_far,
    out_ref,
    tok, send, recv, back, mate, turn_in, side_in, acc_g, acc_u, act, wg, wu, wd, spread, merge, part_ref,
    a_s, a_r, f_s, f_r, d_s, d_r, r_s, r_r, m_s, m_r, n_s, n_r, t_s, t_r, s_s, s_r, w_sem, wd_sem,
):
    sp, ep = lax.axis_index("sp"), lax.axis_index("ep")
    x, core = sp // 2, sp % 2
    z, y = ep // 4, ep % 4
    mine = x % 2
    F = tok.shape[3]
    H = F // 2
    half = wg_own.shape[1]
    rows = send.shape[2]
    tokens = tok.shape[2]
    f32, bf = jnp.float32, jnp.bfloat16

    def x_dev(d):
        return (((x + d) % 4) * 2 + core, ep)

    mate_dev = ((x + 1 - 2 * mine) * 2 + core, ep)

    def offset(m, i):
        return i // 2, (2 * (i % 2) + (i // 2) % 2 + m) % 4

    def plane_dev(m, i, sign):
        dz, dy = offset(m, i)
        return (sp, ((z + sign * dz + 4) % 4) * 4 + (y + sign * dy + 4) % 4)

    seats = [(q // 8, q % 8) for q in range(1, 16)]
    order = [next(q for q in seats if offset(*q) == o) for o in PLANE]

    barrier = pltpu.get_barrier_semaphore()
    for d in LINE:
        pl.semaphore_signal(barrier, inc=1, device_id=x_dev(d), device_id_type=MESH)
    for m, i in order:
        pl.semaphore_signal(barrier, inc=1, device_id=plane_dev(m, i, 1), device_id_type=MESH)

    def shared(c):
        return (c % 2 == 1) & (c < 2 * SHARED)

    def cols(c):
        return pl.ds(pl.multiple_of(c * F, F), F)

    def seat(i):
        return pl.ds(i * BLOCK_SLOTS, BLOCK_SLOTS)

    def w_copies(k):
        s = k % W_SLOTS
        return [
            pltpu.make_async_copy(src.at[cols(k), :], dst.at[s, :, pl.ds(at, half)], w_sem.at[s, i])
            for i, (src, dst, at) in enumerate(
                ((wg_own, wg, 0), (wg_far, wg, half), (wu_own, wu, 0), (wu_far, wu, half))
            )
        ]

    def wd_copies(k):
        s = k % D_SLOTS
        return [
            pltpu.make_async_copy(src.at[:, cols(k)], wd.at[s, pl.ds(at, half), :], wd_sem.at[s, i])
            for i, (src, at) in enumerate(((wd_own, 0), (wd_far, half)))
        ]

    def near_copy(c, i):
        return pltpu.make_async_remote_copy(
            moe_ref.at[:, cols(c)], tok.at[c, x], a_s.at[c, i], a_r.at[c, i],
            device_id=x_dev((1, 3)[i]), device_id_type=MESH,
        )

    def pass_copy(c, i):
        block = tok.at[c, (x + (1, 3)[i]) % 4, :, pl.ds(i * H, H)]
        return pltpu.make_async_remote_copy(
            block, block, f_s.at[c, i], f_r.at[c, i], device_id=x_dev((3, 1)[i]), device_id_type=MESH
        )

    def seat_copy(c, m, i, dst, s_sem, r_sem, sign):
        return pltpu.make_async_remote_copy(
            send.at[c, m, seat(i)], dst.at[c, m, seat(i)], s_sem.at[c, m * 8 + i], r_sem.at[c, m * 8 + i],
            device_id=plane_dev(m, i, sign), device_id_type=MESH,
        )

    def seat_copies(c, way, act_on):
        args = (recv, d_s, d_r, 1) if way == 0 else (back, r_s, r_r, -1)

        @pl.when(shared(c))
        def _():
            for i in SET_ORDER:
                act_on(seat_copy(c, mine, i, *args))

            @pl.when(mine == 1)
            def _():
                act_on(seat_copy(c, mine, 0, *args))

        @pl.when(jnp.logical_not(shared(c)))
        def _():
            for m, i in order:
                act_on(seat_copy(c, m, i, *args))

    def start(copy):
        copy.start()

    def wait_recv(copy):
        copy.wait_recv()

    def wait_send(copy):
        copy.wait_send()

    def mate_rows(c):
        return pltpu.make_async_remote_copy(
            recv.at[c, mine], recv.at[c, mine], m_s.at[c], m_r.at[c], device_id=mate_dev, device_id_type=MESH
        )

    def mate_sums(c):
        return pltpu.make_async_remote_copy(
            send.at[c, 1 - mine], mate.at[c // 2], n_s.at[c], n_r.at[c], device_id=mate_dev, device_id_type=MESH
        )

    def turn_copy(c, i):
        return pltpu.make_async_remote_copy(
            tok.at[c, 0, :, pl.ds(i * H, H)], turn_in.at[c, i], t_s.at[c, i], t_r.at[c, i],
            device_id=x_dev((3, 1)[i]), device_id_type=MESH,
        )

    def side_copy(c, i):
        return pltpu.make_async_remote_copy(
            tok.at[c, 1 + i], side_in.at[c, i], s_s.at[c, i], s_r.at[c, i],
            device_id=x_dev((3, 1)[i]), device_id_type=MESH,
        )

    pl.semaphore_wait(barrier, len(LINE) + len(PLANE))

    @pl.loop(0, chunks)
    def _(c):
        for i in range(2):
            near_copy(c, i).start()

    for k in range(W_SLOTS):
        for cp in w_copies(k):
            cp.start()
    for k in range(D_SLOTS):
        for cp in wd_copies(k):
            cp.start()

    row = lax.broadcasted_iota(jnp.int32, (rows, 1), 0)
    place, rest = row // BLOCK_SLOTS, row % BLOCK_SLOTS
    block, slot = rest // CAP, rest % CAP
    for m in range(2):
        dz, dy = offset(m, place)
        pair = ((z + dz) % 4) * 4 + (y + dy) % 4
        wanted = (2 * pair + x // 2) * CAP + slot
        for b in range(4):
            at = slice(b * tokens, (b + 1) * tokens)
            key = jnp.where(block == b, wanted, -1).astype(f32)
            first = packs_ref[b, 0:1, :] == key
            second = packs_ref[b, 1:2, :] == key
            spread[m, :, at] = jnp.where(first | second, 1.0, 0.0).astype(bf)
            weight = jnp.where(first, packs_ref[b, 2:3, :], 0.0) + jnp.where(second, packs_ref[b, 3:4, :], 0.0)
            merge[m, at, :] = weight.T.astype(bf)

    acc_g[...] = jnp.zeros_like(acc_g)
    acc_u[...] = jnp.zeros_like(acc_u)

    def pass_on(c):
        for i in range(2):
            near_copy(c, 1 - i).wait_recv()
            pass_copy(c, i).start()

    pass_on(0)

    @pl.loop(0, chunks + 3)
    def _(step):
        @pl.when(step + 1 < chunks)
        def _():
            pass_on(step + 1)

        @pl.when(step < chunks)
        def _():
            c = step
            tok[c, x] = moe_ref[:, cols(c)]
            for i in range(2):
                pass_copy(c, i).wait_recv()
            lines = tok[c].reshape(4 * tokens, F)

            @pl.loop(0, 2)
            def _(m):
                @pl.when(jnp.logical_not(shared(c)) | (m == mine))
                def _():
                    send[c, m] = jnp.dot(spread[m], lines, preferred_element_type=f32).astype(bf)

            seat_copies(c, 0, start)

            @pl.when(jnp.logical_not(shared(c)) | (mine == 0))
            def _():
                recv[c, 0, seat(0)] = send[c, 0, seat(0)]

        @pl.when(step >= 3)
        def _():
            k = step - 3
            s = k % W_SLOTS
            for cp in w_copies(k):
                cp.wait()

            @pl.when(shared(k))
            def _():
                mate_rows(k).wait_recv()

            @pl.when(jnp.logical_not(shared(k)))
            def _():
                for m, i in order:
                    seat_copy(k, m, i, recv, d_s, d_r, 1).wait_recv()

            @pl.loop(0, 2)
            def _(m):
                lines = recv[k, m]
                acc_g[m] += jnp.dot(lines, wg[s], preferred_element_type=f32)
                acc_u[m] += jnp.dot(lines, wu[s], preferred_element_type=f32)

            @pl.when(k + W_SLOTS < chunks)
            def _():
                for cp in w_copies(k + W_SLOTS):
                    cp.start()

        @pl.when((step >= 2) & shared(step - 2))
        def _():
            k = step - 2
            for i in SET_ORDER:
                seat_copy(k, mine, i, recv, d_s, d_r, 1).wait_recv()

            @pl.when(mine == 1)
            def _():
                seat_copy(k, mine, 0, recv, d_s, d_r, 1).wait_recv()

            mate_rows(k).start()

    @pl.loop(0, 2 * rows // 64)
    def _(t):
        m, at = t // (rows // 64), pl.ds(pl.multiple_of((t % (rows // 64)) * 64, 64), 64)
        g = acc_g[m, at, :]
        act[m, at, :] = (g / (1.0 + jnp.exp(-g)) * acc_u[m, at, :]).astype(bf)

    def part(k, b):
        at = pl.ds(pl.multiple_of(b * tokens, tokens), tokens)
        part_ref[...] = jnp.dot(merge[mine, at, :], back[k, mine], preferred_element_type=f32)

        @pl.when(jnp.logical_not(shared(k)))
        def _():
            part_ref[...] += jnp.dot(merge[1 - mine, at, :], back[k, 1 - mine], preferred_element_type=f32)

        return part_ref[...]

    @pl.loop(0, chunks + 6)
    def _(step):
        @pl.when(step < chunks)
        def _():
            c = step
            s = c % D_SLOTS
            for cp in wd_copies(c):
                cp.wait()
            seat_copies(c, 0, wait_send)

            @pl.loop(0, 2)
            def _(m):
                @pl.when(jnp.logical_not(shared(c)) | (m != mine))
                def _():
                    send[c, m] = jnp.dot(act[m], wd[s], preferred_element_type=f32).astype(bf)

            @pl.when(shared(c))
            def _():
                mate_sums(c).start()

            @pl.when(jnp.logical_not(shared(c)))
            def _():
                for m, i in order:
                    seat_copy(c, m, i, back, r_s, r_r, -1).start()
                back[c, 0, seat(0)] = send[c, 0, seat(0)]

        @pl.when((step >= 1) & (step < chunks + 1))
        def _():
            k = step - 1

            @pl.when(shared(k))
            def _():
                mate_sums(k).wait_recv()
                both = jnp.dot(act[mine], wd[k % D_SLOTS], preferred_element_type=f32) + mate[k // 2].astype(f32)
                send[k, mine] = both.astype(bf)
                for i in SET_ORDER:
                    seat_copy(k, mine, i, back, r_s, r_r, -1).start()

                @pl.when(mine == 1)
                def _():
                    seat_copy(k, mine, 0, back, r_s, r_r, -1).start()

                @pl.when(mine == 0)
                def _():
                    back[k, 0, seat(0)] = send[k, 0, seat(0)]

            @pl.when(k + D_SLOTS < chunks)
            def _():
                for cp in wd_copies(k + D_SLOTS):
                    cp.start()

        @pl.when((step >= 3) & (step < chunks + 3))
        def _():
            k = step - 3
            seat_copies(k, 1, wait_recv)
            for i in range(2):
                pass_copy(k, i).wait_send()
            tok[k, 0] = part(k, (x + 2) % 4).astype(bf)
            for i in range(2):
                turn_copy(k, i).start()

        @pl.when((step >= 4) & (step < chunks + 4))
        def _():
            k = step - 4
            for i in range(2):
                near = slice(i * H, (i + 1) * H)
                rest = slice((1 - i) * H, (2 - i) * H)
                side = part(k, (x + (3, 1)[i]) % 4)
                turn_copy(k, i).wait_recv()
                tok[k, 1 + i, :, near] = (side[:, near] + turn_in[k, i].astype(f32)).astype(bf)
                tok[k, 1 + i, :, rest] = side[:, rest].astype(bf)
                side_copy(k, i).start()

        @pl.when(step >= 6)
        def _():
            k = step - 6
            total = part(k, x)
            for i in range(2):
                side_copy(k, i).wait_recv()
                total = total + side_in[k, i].astype(f32)
            out_ref[:, cols(k)] = (res_ref[:, cols(k)] + mod_ref[3:4, cols(k)] * total).astype(out_ref.dtype)

    @pl.loop(0, chunks)
    def _(c):
        for i in range(2):
            near_copy(c, i).wait_send()
            turn_copy(c, i).wait_send()
            side_copy(c, i).wait_send()
        seat_copies(c, 1, wait_send)

        @pl.when(shared(c))
        def _():
            mate_rows(c).wait_send()
            mate_sums(c).wait_send()


def experts(moe_in, residual, modulation, packs, weights):
    tokens, width = moe_in.shape
    chunks = 8
    F = width // chunks
    rows = 8 * BLOCK_SLOTS
    hidden = 2 * weights[0].shape[1]
    bf, f32 = jnp.bfloat16, jnp.float32
    dma = pltpu.SemaphoreType.DMA
    vmem = pl.BlockSpec(memory_space=pltpu.VMEM)
    hbm = pl.BlockSpec(memory_space=pl.ANY)
    return pl.pallas_call(
        functools.partial(expert_kernel, chunks),
        out_shape=jax.ShapeDtypeStruct((tokens, width), bf),
        in_specs=[vmem] * 4 + [hbm] * 6,
        out_specs=vmem,
        scratch_shapes=[
            pltpu.VMEM((chunks, 4, tokens, F), bf),
            pltpu.VMEM((chunks, 2, rows, F), bf),
            pltpu.VMEM((chunks, 2, rows, F), bf),
            pltpu.VMEM((chunks, 2, rows, F), bf),
            pltpu.VMEM((SHARED, rows, F), bf),
            pltpu.VMEM((chunks, 2, tokens, F // 2), bf),
            pltpu.VMEM((chunks, 2, tokens, F), bf),
            pltpu.VMEM((2, rows, hidden), f32),
            pltpu.VMEM((2, rows, hidden), f32),
            pltpu.VMEM((2, rows, hidden), bf),
            pltpu.VMEM((W_SLOTS, F, hidden), bf),
            pltpu.VMEM((W_SLOTS, F, hidden), bf),
            pltpu.VMEM((D_SLOTS, hidden, F), bf),
            pltpu.VMEM((2, rows, 4 * tokens), bf),
            pltpu.VMEM((2, 4 * tokens, rows), bf),
            pltpu.VMEM((tokens, F), f32),
        ]
        + [dma((chunks, 2))] * 4
        + [dma((chunks, 16))] * 4
        + [dma((chunks,))] * 4
        + [dma((chunks, 2))] * 4
        + [dma((W_SLOTS, 4)), dma((D_SLOTS, 2))],
        compiler_params=pltpu.CompilerParams(
            collective_id=0, has_side_effects=True, vmem_limit_bytes=62 * 1024 * 1024
        ),
        cost_estimate=pl.CostEstimate(flops=26_000_000_000, bytes_accessed=40_000_000, transcendentals=800_000),
        name="experts",
    )(moe_in, residual, modulation, packs, *weights)


def local(
    latent,
    attention_in,
    out_weight,
    modulation,
    route_experts,
    route_slots,
    route_gates,
    gate_weight,
    up_weight,
    down_weight,
):
    weights = [gate_weight[0], up_weight[0], down_weight[0]]
    routes = [route_experts[0].T, route_slots[0].T, route_gates[0].T]
    qkv = jnp.transpose(attention_in[0], (1, 0, 2))
    moe_in, residual, packs, far = attention(qkv, latent[0], out_weight, modulation, routes, weights)
    both = [w for pair in zip(weights, far) for w in pair]
    return experts(moe_in, residual, modulation, packs, both)[None]


def solution(mesh):
    return jax.shard_map(
        local,
        mesh=mesh,
        in_specs=(
            P("ep", "sp", None),
            P("ep", "sp", None, None),
            P("sp", None),
            P(),
            P("ep", "sp", None),
            P("ep", "sp", None),
            P("ep", "sp", None),
            P("ep", None, "sp"),
            P("ep", None, "sp"),
            P("ep", "sp", None),
        ),
        out_specs=P("ep", "sp", None),
        check_vma=False,
    )
```

```python
import functools
import math

import jax
import jax.numpy as jnp
from jax import lax
from jax.experimental import pallas as pl
from jax.experimental.pallas import tpu as pltpu
from jax.sharding import PartitionSpec as P

HD = 128
MESH = pl.DeviceIdType.MESH

PLANE = (
    (1, 0), (0, 1), (3, 0), (0, 3), (1, 1), (3, 3), (2, 0), (0, 2),
    (1, 3), (3, 1), (2, 1), (1, 2), (2, 3), (3, 2), (2, 2),
)
LINE = (1, 3, 2)
CAP = 12
BLOCK_SLOTS = 4 * CAP
FAR_LATE = 8
W_SLOTS = 3
D_SLOTS = 5
SHARED = 3
SET_ORDER = (1, 2, 4, 7, 3, 6, 5)


def attention_kernel(
    chunks,
    qkv_ref, latent_hbm, wo_hbm, mod_ref, experts_ref, slots_ref, gates_ref, wg_ref, wu_ref, wd_ref,
    moe_hbm, res_hbm, packs_ref, wg_far, wu_far, wd_far,
    latent_ref, wo_ref, moe_ref, res_ref, pack_ref, heads, values, att, pair_out, pair_in, turn_out, turn_in, side, side_out, side_in, own,
    q_s, q_r, q_l, p_s, p_r, t_s, t_r, s_s, s_r, w_s, w_r, k_s, k_r, k_l, in_sem, moe_sem, res_sem,
):
    sp, ep = lax.axis_index("sp"), lax.axis_index("ep")
    x, core = sp // 2, sp % 2
    n_heads, _, window, hd = heads.shape
    tokens = window // 8
    F = wo_ref.shape[1] // chunks
    H = F // 2
    f32, bf = jnp.float32, jnp.bfloat16

    def x_peer(d):
        return (x + d) % 4

    def x_dev(d):
        return (x_peer(d) * 2 + core, ep)

    partner = (x * 2 + 1 - core, ep)
    others = [(d, k) for d in (2, 1, 3, 0) for k in (0, 1) if (d, k) != (0, 0)]

    def other(i):
        d, k = others[i]
        return x_peer(d) * 2 + (core + k) % 2

    def cols(c):
        return pl.ds(pl.multiple_of(c * F, F), F)

    def block(s):
        return pl.ds(pl.multiple_of(s * tokens, tokens), tokens)

    def head_cols(s, h):
        return pl.ds(pl.multiple_of((s * n_heads + h) * hd, hd), hd)

    def head_copy(h, i):
        to = other(i)
        return pltpu.make_async_remote_copy(
            qkv_ref.at[:, :, head_cols(to, h)], heads.at[h, :, block(sp), :], q_s.at[h, i], q_r.at[h, i],
            device_id=(to, ep), device_id_type=MESH,
        )

    def head_local(h):
        return pltpu.make_async_copy(
            qkv_ref.at[:, :, head_cols(sp, h)], heads.at[h, :, block(sp), :], q_l.at[h]
        )

    def weight_copy(i):
        src, dst = ((wg_ref, wg_far), (wu_ref, wu_far), (wd_ref, wd_far))[i]
        return pltpu.make_async_remote_copy(
            src, dst, w_s.at[i], w_r.at[i], device_id=partner, device_id_type=MESH
        )

    def pack_copy(i):
        return pltpu.make_async_remote_copy(
            pack_ref, packs_ref.at[x], k_s.at[i], k_r.at[i], device_id=x_dev(LINE[i]), device_id_type=MESH
        )

    pack_local = pltpu.make_async_copy(pack_ref, packs_ref.at[x], k_l)

    def pair_copy(c):
        return pltpu.make_async_remote_copy(
            pair_out.at[c], pair_in.at[c], p_s.at[c], p_r.at[c], device_id=partner, device_id_type=MESH
        )

    def turn_copy(c, i):
        return pltpu.make_async_remote_copy(
            turn_out.at[c, i], turn_in.at[c, i], t_s.at[c, i], t_r.at[c, i],
            device_id=x_dev((3, 1)[i]), device_id_type=MESH,
        )

    def side_copy(c, i):
        return pltpu.make_async_remote_copy(
            side_out.at[c, i], side_in.at[c, i], s_s.at[c, i], s_r.at[c, i],
            device_id=x_dev((3, 1)[i]), device_id_type=MESH,
        )

    loads = [
        pltpu.make_async_copy(wo_hbm, wo_ref, in_sem.at[0]),
        pltpu.make_async_copy(latent_hbm, latent_ref, in_sem.at[1]),
    ]

    def moe_copy(m):
        at = pl.ds(pl.multiple_of(m * 16, 16), 16)
        return pltpu.make_async_copy(moe_ref.at[at, :], moe_hbm.at[at, :], moe_sem.at[m])

    def res_copy(c):
        return pltpu.make_async_copy(res_ref.at[:, cols(c)], res_hbm.at[:, cols(c)], res_sem.at[c])

    barrier = pltpu.get_barrier_semaphore()
    for i in range(7):
        pl.semaphore_signal(barrier, inc=1, device_id=(other(i), ep), device_id_type=MESH)
    for h in range(n_heads):
        head_local(h).start()
    pack_ref[0:2, :] = (experts_ref[...] * CAP + slots_ref[...]).astype(f32)
    pack_ref[2:4, :] = gates_ref[...]
    pack_ref[4:8, :] = jnp.zeros((4, tokens), f32)
    pack_local.start()
    pl.semaphore_wait(barrier, 7)

    @pl.loop(0, n_heads)
    def _(h):
        for i in range(7):
            head_copy(h, i).start()

    for i in range(3):
        pack_copy(i).start()
    for i in range(3):
        weight_copy(i).start()

    for cp in loads:
        cp.start()
    values[:, hd:] = jnp.ones((window, hd), bf)
    factor = math.log2(math.e) / math.sqrt(hd)
    q_tile = 2 * tokens

    @pl.loop(0, n_heads)
    def _(h):
        head_local(h).wait()
        for i in range(7):
            head_copy(h, i).wait_recv()
        values[:, :hd] = heads[h, 2]

        @pl.loop(0, window // q_tile)
        def _(m):
            at = pl.ds(pl.multiple_of(m * q_tile, q_tile), q_tile)
            scores = lax.dot_general(
                heads[h, 0, at, :], heads[h, 1], (((1,), (1,)), ((), ())), preferred_element_type=f32
            )
            top = jnp.max(scores, axis=1, keepdims=True)
            lifted = jnp.exp2((scores - top) * factor).astype(bf)
            mixed = jnp.dot(lifted, values[...], preferred_element_type=f32)
            out = (mixed[:, :hd] / mixed[:, hd:]).astype(bf)
            to = (block(m), pl.ds(pl.multiple_of(h * hd, hd), hd))
            att[0, to[0], to[1]] = out[:tokens]
            att[1, to[0], to[1]] = out[tokens:]

    for cp in loads:
        cp.wait()

    far_at = (1 - core) * FAR_LATE
    sum_at = 1 + core * (chunks - 1)

    @pl.loop(0, 2 * chunks + 5)
    def _(step):
        @pl.when((step >= far_at) & (step < far_at + chunks))
        def _():
            c = step - far_at
            far = jnp.dot(att[1 - core], wo_ref[:, cols(c)], preferred_element_type=f32)
            pair_out[c] = far.astype(bf)
            pair_copy(c).start()

        @pl.when((step >= sum_at) & (step < sum_at + chunks))
        def _():
            c = step - sum_at
            pair_copy(c).wait_recv()

            def part(b):
                return jnp.dot(
                    att[core, block(b), :], wo_ref[:, cols(c)], preferred_element_type=f32
                ) + pair_in[c, block(b), :].astype(f32)

            over = part(x_peer(2)).astype(bf)
            for i in range(2):
                turn_out[c, i] = over[:, i * H : (i + 1) * H]
                turn_copy(c, i).start()
            side[c, 0] = part(x_peer(3))
            side[c, 1] = part(x_peer(1))
            own[c] = part(x)

        @pl.when((step >= sum_at + 2) & (step < sum_at + chunks + 2))
        def _():
            c = step - sum_at - 2
            for i in range(2):
                turn_copy(c, i).wait_recv()
                near = slice(i * H, (i + 1) * H)
                rest = slice((1 - i) * H, (2 - i) * H)
                side_out[c, i, :, near] = (side[c, i, :, near] + turn_in[c, i].astype(f32)).astype(bf)
                side_out[c, i, :, rest] = side[c, i, :, rest].astype(bf)
                side_copy(c, i).start()

        @pl.when((step >= sum_at + 5) & (step < sum_at + chunks + 5))
        def _():
            c = step - sum_at - 5
            total = own[c]
            for i in range(2):
                side_copy(c, i).wait_recv()
                total = total + side_in[c, i].astype(f32)
            res_ref[:, cols(c)] = latent_ref[:, cols(c)].astype(f32) + mod_ref[0:1, cols(c)] * total
            res_copy(c).start()

    @pl.loop(0, tokens // 16)
    def _(m):
        at = pl.ds(pl.multiple_of(m * 16, 16), 16)
        rows = res_ref[at, :]
        centered = rows - jnp.mean(rows, axis=1, keepdims=True)
        variance = jnp.mean(centered * centered, axis=1, keepdims=True)
        normed = centered * lax.rsqrt(variance + 1e-06)
        moe_ref[at, :] = (normed * (1.0 + mod_ref[2:3, :]) + mod_ref[1:2, :]).astype(bf)
        moe_copy(m).start()

    @pl.loop(0, tokens // 16)
    def _(m):
        moe_copy(m).wait()

    pack_local.wait()
    for i in range(3):
        pack_copy(i).wait()
        weight_copy(i).wait()

    @pl.loop(0, n_heads)
    def _(h):
        for i in range(7):
            head_copy(h, i).wait_send()

    @pl.loop(0, chunks)
    def _(c):
        res_copy(c).wait()
        pair_copy(c).wait_send()
        for i in range(2):
            turn_copy(c, i).wait_send()
            side_copy(c, i).wait_send()


def attention(qkv, latent, out_weight, modulation, routes, weights):
    tokens, width = latent.shape
    chunks = 8
    F = width // chunks
    group = out_weight.shape[0]
    window = 8 * tokens
    bf, f32 = jnp.bfloat16, jnp.float32
    dma = pltpu.SemaphoreType.DMA
    vmem = pl.BlockSpec(memory_space=pltpu.VMEM)
    hbm = pl.BlockSpec(memory_space=pl.ANY)
    outs = pl.pallas_call(
        functools.partial(attention_kernel, chunks),
        out_shape=[
            jax.ShapeDtypeStruct((tokens, width), bf),
            jax.ShapeDtypeStruct((tokens, width), f32),
            jax.ShapeDtypeStruct((4, 8, tokens), f32),
        ]
        + [jax.ShapeDtypeStruct(w.shape, bf) for w in weights],
        in_specs=[hbm] * 3 + [vmem] * 4 + [hbm] * 3,
        out_specs=[hbm] * 6,
        scratch_shapes=[
            pltpu.VMEM((tokens, width), bf),
            pltpu.VMEM((group, width), bf),
            pltpu.VMEM((tokens, width), bf),
            pltpu.VMEM((tokens, width), f32),
            pltpu.VMEM((8, tokens), f32),
            pltpu.VMEM((group // HD, 3, window, HD), bf),
            pltpu.VMEM((window, 2 * HD), bf),
            pltpu.VMEM((2, window // 2, group), bf),
            pltpu.VMEM((chunks, window // 2, F), bf),
            pltpu.VMEM((chunks, window // 2, F), bf),
            pltpu.VMEM((chunks, 2, tokens, F // 2), bf),
            pltpu.VMEM((chunks, 2, tokens, F // 2), bf),
            pltpu.VMEM((chunks, 2, tokens, F), f32),
            pltpu.VMEM((chunks, 2, tokens, F), bf),
            pltpu.VMEM((chunks, 2, tokens, F), bf),
            pltpu.VMEM((chunks, tokens, F), f32),
            dma((4, 7)), dma((4, 7)), dma((4,)),
            dma((chunks,)), dma((chunks,)),
            dma((chunks, 2)), dma((chunks, 2)),
            dma((chunks, 2)), dma((chunks, 2)),
            dma((3,)), dma((3,)), dma((3,)), dma((3,)), dma,
            dma((2,)), dma((tokens // 16,)), dma((chunks,)),
        ],
        compiler_params=pltpu.CompilerParams(
            collective_id=1, has_side_effects=True, vmem_limit_bytes=60 * 1024 * 1024
        ),
        cost_estimate=pl.CostEstimate(flops=6_500_000_000, bytes_accessed=40_000_000, transcendentals=4_200_000),
        name="attention",
    )(qkv, latent, out_weight, modulation, *routes, *weights)
    return outs[0], outs[1], outs[2], outs[3:]


def expert_kernel(
    chunks,
    moe_ref, res_hbm, mod_ref, packs_ref, wg_own, wg_far, wu_own, wu_far, wd_own, wd_far,
    out_ref,
    tok, send, recv, back, mate, turn_in, side_in, acc_g, acc_u, act, wg, wu, wd, spread, merge, part_ref, res_ref,
    a_s, a_r, f_s, f_r, d_s, d_r, r_s, r_r, m_s, m_r, n_s, n_r, t_s, t_r, s_s, s_r, w_sem, wd_sem, own_sem, res_sem,
):
    sp, ep = lax.axis_index("sp"), lax.axis_index("ep")
    x, core = sp // 2, sp % 2
    z, y = ep // 4, ep % 4
    mine = x % 2
    F = tok.shape[3]
    H = F // 2
    half = wg_own.shape[1]
    rows = send.shape[2]
    tokens = tok.shape[2]
    f32, bf = jnp.float32, jnp.bfloat16

    def x_dev(d):
        return (((x + d) % 4) * 2 + core, ep)

    mate_dev = ((x + 1 - 2 * mine) * 2 + core, ep)

    def offset(m, i):
        return i // 2, (2 * (i % 2) + (i // 2) % 2 + m) % 4

    def plane_dev(m, i, sign):
        dz, dy = offset(m, i)
        return (sp, ((z + sign * dz + 4) % 4) * 4 + (y + sign * dy + 4) % 4)

    seats = [(q // 8, q % 8) for q in range(1, 16)]
    order = [next(q for q in seats if offset(*q) == o) for o in PLANE]

    barrier = pltpu.get_barrier_semaphore()
    for d in LINE:
        pl.semaphore_signal(barrier, inc=1, device_id=x_dev(d), device_id_type=MESH)
    for m, i in order:
        pl.semaphore_signal(barrier, inc=1, device_id=plane_dev(m, i, 1), device_id_type=MESH)

    def shared(c):
        return (c % 2 == 1) & (c < 2 * SHARED)

    def cols(c):
        return pl.ds(pl.multiple_of(c * F, F), F)

    def seat(i):
        return pl.ds(i * BLOCK_SLOTS, BLOCK_SLOTS)

    def w_copies(k):
        s = k % W_SLOTS
        return [
            pltpu.make_async_copy(src.at[cols(k), :], dst.at[s, :, pl.ds(at, half)], w_sem.at[s, i])
            for i, (src, dst, at) in enumerate(
                ((wg_own, wg, 0), (wg_far, wg, half), (wu_own, wu, 0), (wu_far, wu, half))
            )
        ]

    def wd_copies(k):
        s = k % D_SLOTS
        return [
            pltpu.make_async_copy(src.at[:, cols(k)], wd.at[s, pl.ds(at, half), :], wd_sem.at[s, i])
            for i, (src, at) in enumerate(((wd_own, 0), (wd_far, half)))
        ]

    def own_copy(c):
        return pltpu.make_async_copy(moe_ref.at[:, cols(c)], tok.at[c, x], own_sem.at[c])

    res_copy = pltpu.make_async_copy(res_hbm, res_ref, res_sem)

    def near_copy(c, i):
        return pltpu.make_async_remote_copy(
            moe_ref.at[:, cols(c)], tok.at[c, x], a_s.at[c, i], a_r.at[c, i],
            device_id=x_dev((1, 3)[i]), device_id_type=MESH,
        )

    def pass_copy(c, i):
        block = tok.at[c, (x + (1, 3)[i]) % 4, :, pl.ds(i * H, H)]
        return pltpu.make_async_remote_copy(
            block, block, f_s.at[c, i], f_r.at[c, i], device_id=x_dev((3, 1)[i]), device_id_type=MESH
        )

    def seat_copy(c, m, i, dst, s_sem, r_sem, sign):
        return pltpu.make_async_remote_copy(
            send.at[c, m, seat(i)], dst.at[c, m, seat(i)], s_sem.at[c, m * 8 + i], r_sem.at[c, m * 8 + i],
            device_id=plane_dev(m, i, sign), device_id_type=MESH,
        )

    def seat_copies(c, way, act_on):
        args = (recv, d_s, d_r, 1) if way == 0 else (back, r_s, r_r, -1)

        @pl.when(shared(c))
        def _():
            for i in SET_ORDER:
                act_on(seat_copy(c, mine, i, *args))

            @pl.when(mine == 1)
            def _():
                act_on(seat_copy(c, mine, 0, *args))

        @pl.when(jnp.logical_not(shared(c)))
        def _():
            for m, i in order:
                act_on(seat_copy(c, m, i, *args))

    def start(copy):
        copy.start()

    def wait_recv(copy):
        copy.wait_recv()

    def wait_send(copy):
        copy.wait_send()

    def mate_rows(c):
        return pltpu.make_async_remote_copy(
            recv.at[c, mine], recv.at[c, mine], m_s.at[c], m_r.at[c], device_id=mate_dev, device_id_type=MESH
        )

    def mate_sums(c):
        return pltpu.make_async_remote_copy(
            send.at[c, 1 - mine], mate.at[c // 2], n_s.at[c], n_r.at[c], device_id=mate_dev, device_id_type=MESH
        )

    def turn_copy(c, i):
        return pltpu.make_async_remote_copy(
            tok.at[c, 0, :, pl.ds(i * H, H)], turn_in.at[c, i], t_s.at[c, i], t_r.at[c, i],
            device_id=x_dev((3, 1)[i]), device_id_type=MESH,
        )

    def side_copy(c, i):
        return pltpu.make_async_remote_copy(
            tok.at[c, 1 + i], side_in.at[c, i], s_s.at[c, i], s_r.at[c, i],
            device_id=x_dev((3, 1)[i]), device_id_type=MESH,
        )

    pl.semaphore_wait(barrier, len(LINE) + len(PLANE))

    @pl.loop(0, 2)
    def _(c):
        for i in range(2):
            near_copy(c, i).start()

    @pl.loop(0, chunks)
    def _(c):
        own_copy(c).start()

    for k in range(W_SLOTS):
        for cp in w_copies(k):
            cp.start()
    for k in range(D_SLOTS):
        for cp in wd_copies(k):
            cp.start()
    res_copy.start()

    row = lax.broadcasted_iota(jnp.int32, (rows, 1), 0)
    place, rest = row // BLOCK_SLOTS, row % BLOCK_SLOTS
    block, slot = rest // CAP, rest % CAP
    for m in range(2):
        dz, dy = offset(m, place)
        pair = ((z + dz) % 4) * 4 + (y + dy) % 4
        wanted = (2 * pair + x // 2) * CAP + slot
        for b in range(4):
            at = slice(b * tokens, (b + 1) * tokens)
            key = jnp.where(block == b, wanted, -1).astype(f32)
            first = packs_ref[b, 0:1, :] == key
            second = packs_ref[b, 1:2, :] == key
            spread[m, :, at] = jnp.where(first | second, 1.0, 0.0).astype(bf)
            weight = jnp.where(first, packs_ref[b, 2:3, :], 0.0) + jnp.where(second, packs_ref[b, 3:4, :], 0.0)
            merge[m, at, :] = weight.T.astype(bf)

    acc_g[...] = jnp.zeros_like(acc_g)
    acc_u[...] = jnp.zeros_like(acc_u)

    def pass_on(c):
        for i in range(2):
            near_copy(c, 1 - i).wait_recv()
            pass_copy(c, i).start()

        @pl.when(c + 2 < chunks)
        def _():
            for i in range(2):
                near_copy(c + 2, i).start()

    pass_on(0)

    @pl.loop(0, chunks + 2)
    def _(step):
        @pl.when(step + 1 < chunks)
        def _():
            pass_on(step + 1)

        @pl.when(step < chunks)
        def _():
            c = step
            own_copy(c).wait()
            for i in range(2):
                pass_copy(c, i).wait_recv()
            lines = tok[c].reshape(4 * tokens, F)

            @pl.loop(0, 2)
            def _(m):
                @pl.when(jnp.logical_not(shared(c)) | (m == mine))
                def _():
                    send[c, m] = jnp.dot(spread[m], lines, preferred_element_type=f32).astype(bf)

            seat_copies(c, 0, start)

            @pl.when(jnp.logical_not(shared(c)) | (mine == 0))
            def _():
                recv[c, 0, seat(0)] = send[c, 0, seat(0)]

        @pl.when(step >= 3)
        def _():
            k = step - 3
            s = k % W_SLOTS
            for cp in w_copies(k):
                cp.wait()

            @pl.when(shared(k))
            def _():
                mate_rows(k).wait_recv()

            @pl.when(jnp.logical_not(shared(k)))
            def _():
                for m, i in order:
                    seat_copy(k, m, i, recv, d_s, d_r, 1).wait_recv()

            @pl.loop(0, 2)
            def _(m):
                lines = recv[k, m]
                acc_g[m] += jnp.dot(lines, wg[s], preferred_element_type=f32)
                acc_u[m] += jnp.dot(lines, wu[s], preferred_element_type=f32)

            @pl.when(k + W_SLOTS < chunks)
            def _():
                for cp in w_copies(k + W_SLOTS):
                    cp.start()

        @pl.when((step >= 2) & shared(step - 2))
        def _():
            k = step - 2
            for i in SET_ORDER:
                seat_copy(k, mine, i, recv, d_s, d_r, 1).wait_recv()

            @pl.when(mine == 1)
            def _():
                seat_copy(k, mine, 0, recv, d_s, d_r, 1).wait_recv()

            mate_rows(k).start()

    last = chunks - 1
    for cp in w_copies(last) + wd_copies(0):
        cp.wait()
    seat_copies(last, 0, wait_recv)
    seat_copies(0, 0, wait_send)
    res_copy.wait()

    @pl.loop(0, 2)
    def _(m):
        lines = recv[last, m]
        acc_g[m] += jnp.dot(lines, wg[last % W_SLOTS], preferred_element_type=f32)
        acc_u[m] += jnp.dot(lines, wu[last % W_SLOTS], preferred_element_type=f32)

        @pl.loop(0, rows // 64)
        def _(t):
            at = pl.ds(pl.multiple_of(t * 64, 64), 64)
            g = acc_g[m, at, :]
            act[m, at, :] = (g / (1.0 + jnp.exp(-g)) * acc_u[m, at, :]).astype(bf)

        send[0, m] = jnp.dot(act[m], wd[0], preferred_element_type=f32).astype(bf)
        for i in SET_ORDER:
            seat_copy(0, m, i, back, r_s, r_r, -1).start()

        @pl.when(m == 1)
        def _():
            seat_copy(0, m, 0, back, r_s, r_r, -1).start()

        @pl.when(m == 0)
        def _():
            back[0, 0, seat(0)] = send[0, 0, seat(0)]

    def part(k, b):
        at = pl.ds(pl.multiple_of(b * tokens, tokens), tokens)
        part_ref[...] = jnp.dot(merge[mine, at, :], back[k, mine], preferred_element_type=f32)

        @pl.when(jnp.logical_not(shared(k)))
        def _():
            part_ref[...] += jnp.dot(merge[1 - mine, at, :], back[k, 1 - mine], preferred_element_type=f32)

        return part_ref[...]

    @pl.loop(0, chunks + 6)
    def _(step):
        @pl.when((step >= 1) & (step < chunks))
        def _():
            c = step
            s = c % D_SLOTS
            for cp in wd_copies(c):
                cp.wait()
            seat_copies(c, 0, wait_send)

            @pl.loop(0, 2)
            def _(m):
                @pl.when(jnp.logical_not(shared(c)) | (m != mine))
                def _():
                    send[c, m] = jnp.dot(act[m], wd[s], preferred_element_type=f32).astype(bf)

            @pl.when(shared(c))
            def _():
                mate_sums(c).start()

            @pl.when(jnp.logical_not(shared(c)))
            def _():
                for m, i in order:
                    seat_copy(c, m, i, back, r_s, r_r, -1).start()
                back[c, 0, seat(0)] = send[c, 0, seat(0)]

        @pl.when((step >= 1) & (step < chunks + 1))
        def _():
            k = step - 1

            @pl.when(shared(k))
            def _():
                mate_sums(k).wait_recv()
                both = jnp.dot(act[mine], wd[k % D_SLOTS], preferred_element_type=f32) + mate[k // 2].astype(f32)
                send[k, mine] = both.astype(bf)
                for i in SET_ORDER:
                    seat_copy(k, mine, i, back, r_s, r_r, -1).start()

                @pl.when(mine == 1)
                def _():
                    seat_copy(k, mine, 0, back, r_s, r_r, -1).start()

                @pl.when(mine == 0)
                def _():
                    back[k, 0, seat(0)] = send[k, 0, seat(0)]

            @pl.when(k + D_SLOTS < chunks)
            def _():
                for cp in wd_copies(k + D_SLOTS):
                    cp.start()

        @pl.when((step >= 3) & (step < chunks + 3))
        def _():
            k = step - 3
            seat_copies(k, 1, wait_recv)
            for i in range(2):
                pass_copy(k, i).wait_send()
            tok[k, 0] = part(k, (x + 2) % 4).astype(bf)
            for i in range(2):
                turn_copy(k, i).start()

        @pl.when((step >= 4) & (step < chunks + 4))
        def _():
            k = step - 4
            for i in range(2):
                near = slice(i * H, (i + 1) * H)
                rest = slice((1 - i) * H, (2 - i) * H)
                side = part(k, (x + (3, 1)[i]) % 4)
                turn_copy(k, i).wait_recv()
                tok[k, 1 + i, :, near] = (side[:, near] + turn_in[k, i].astype(f32)).astype(bf)
                tok[k, 1 + i, :, rest] = side[:, rest].astype(bf)
                side_copy(k, i).start()

        @pl.when(step >= 6)
        def _():
            k = step - 6
            total = part(k, x)
            for i in range(2):
                side_copy(k, i).wait_recv()
                total = total + side_in[k, i].astype(f32)
            out_ref[:, cols(k)] = (res_ref[:, cols(k)] + mod_ref[3:4, cols(k)] * total).astype(out_ref.dtype)

    @pl.loop(0, chunks)
    def _(c):
        for i in range(2):
            near_copy(c, i).wait_send()
            turn_copy(c, i).wait_send()
            side_copy(c, i).wait_send()
        seat_copies(c, 1, wait_send)

        @pl.when(shared(c))
        def _():
            mate_rows(c).wait_send()
            mate_sums(c).wait_send()


def experts(moe_in, residual, modulation, packs, weights):
    tokens, width = moe_in.shape
    chunks = 8
    F = width // chunks
    rows = 8 * BLOCK_SLOTS
    hidden = 2 * weights[0].shape[1]
    bf, f32 = jnp.bfloat16, jnp.float32
    dma = pltpu.SemaphoreType.DMA
    vmem = pl.BlockSpec(memory_space=pltpu.VMEM)
    hbm = pl.BlockSpec(memory_space=pl.ANY)
    return pl.pallas_call(
        functools.partial(expert_kernel, chunks),
        out_shape=jax.ShapeDtypeStruct((tokens, width), bf),
        in_specs=[hbm] * 2 + [vmem] * 2 + [hbm] * 6,
        out_specs=vmem,
        scratch_shapes=[
            pltpu.VMEM((chunks, 4, tokens, F), bf),
            pltpu.VMEM((chunks, 2, rows, F), bf),
            pltpu.VMEM((chunks, 2, rows, F), bf),
            pltpu.VMEM((chunks, 2, rows, F), bf),
            pltpu.VMEM((SHARED, rows, F), bf),
            pltpu.VMEM((chunks, 2, tokens, F // 2), bf),
            pltpu.VMEM((chunks, 2, tokens, F), bf),
            pltpu.VMEM((2, rows, hidden), f32),
            pltpu.VMEM((2, rows, hidden), f32),
            pltpu.VMEM((2, rows, hidden), bf),
            pltpu.VMEM((W_SLOTS, F, hidden), bf),
            pltpu.VMEM((W_SLOTS, F, hidden), bf),
            pltpu.VMEM((D_SLOTS, hidden, F), bf),
            pltpu.VMEM((2, rows, 4 * tokens), bf),
            pltpu.VMEM((2, 4 * tokens, rows), bf),
            pltpu.VMEM((tokens, F), f32),
            pltpu.VMEM((tokens, width), f32),
        ]
        + [dma((chunks, 2))] * 4
        + [dma((chunks, 16))] * 4
        + [dma((chunks,))] * 4
        + [dma((chunks, 2))] * 4
        + [dma((W_SLOTS, 4)), dma((D_SLOTS, 2)), dma((chunks,)), dma],
        compiler_params=pltpu.CompilerParams(
            collective_id=0, has_side_effects=True, vmem_limit_bytes=62 * 1024 * 1024
        ),
        cost_estimate=pl.CostEstimate(flops=26_000_000_000, bytes_accessed=40_000_000, transcendentals=800_000),
        name="experts",
    )(moe_in, residual, modulation, packs, *weights)


def local(
    latent,
    attention_in,
    out_weight,
    modulation,
    route_experts,
    route_slots,
    route_gates,
    gate_weight,
    up_weight,
    down_weight,
):
    weights = [gate_weight[0], up_weight[0], down_weight[0]]
    routes = [route_experts[0].T, route_slots[0].T, route_gates[0].T]
    qkv = jnp.transpose(attention_in[0], (1, 0, 2))
    moe_in, residual, packs, far = attention(qkv, latent[0], out_weight, modulation, routes, weights)
    both = [w for pair in zip(weights, far) for w in pair]
    return experts(moe_in, residual, modulation, packs, both)[None]


def solution(mesh):
    return jax.shard_map(
        local,
        mesh=mesh,
        in_specs=(
            P("ep", "sp", None),
            P("ep", "sp", None, None),
            P("sp", None),
            P(),
            P("ep", "sp", None),
            P("ep", "sp", None),
            P("ep", "sp", None),
            P("ep", None, "sp"),
            P("ep", None, "sp"),
            P("ep", "sp", None),
        ),
        out_specs=P("ep", "sp", None),
        check_vma=False,
    )
```

```python
import functools
import math

import jax
import jax.numpy as jnp
from jax import lax
from jax.experimental import pallas as pl
from jax.experimental.pallas import tpu as pltpu
from jax.sharding import PartitionSpec as P

HD = 128
MESH = pl.DeviceIdType.MESH

PLANE = (
    (2, 2), (1, 0), (0, 1), (3, 0), (0, 3), (2, 1), (1, 2), (2, 3), (3, 2),
    (1, 1), (3, 3), (2, 0), (0, 2), (1, 3), (3, 1),
)
LINE = (1, 3, 2)
CAP = 12
BLOCK_SLOTS = 4 * CAP
FAR_LATE = 8
W_SLOTS = 3
D_SLOTS = 5
SHARED = 3
SET_ORDER = (1, 2, 4, 7, 3, 6, 5)


def attention_kernel(
    chunks,
    qkv_ref, latent_hbm, wo_hbm, mod_ref, experts_ref, slots_ref, gates_ref, wg_ref, wu_ref, wd_ref,
    moe_hbm, res_hbm, packs_ref, wg_far, wu_far, wd_far,
    latent_ref, wo_ref, moe_ref, res_ref, pack_ref, heads, values, att, pair_out, pair_in, turn_out, turn_in, side, side_out, side_in, own,
    q_s, q_r, q_l, p_s, p_r, t_s, t_r, s_s, s_r, w_s, w_r, k_s, k_r, k_l, in_sem, moe_sem, res_sem,
):
    sp, ep = lax.axis_index("sp"), lax.axis_index("ep")
    x, core = sp // 2, sp % 2
    n_heads, _, window, hd = heads.shape
    tokens = window // 8
    F = wo_ref.shape[1] // chunks
    H = F // 2
    f32, bf = jnp.float32, jnp.bfloat16

    def x_peer(d):
        return (x + d) % 4

    def x_dev(d):
        return (x_peer(d) * 2 + core, ep)

    partner = (x * 2 + 1 - core, ep)
    others = [(d, k) for d in (2, 1, 3, 0) for k in (0, 1) if (d, k) != (0, 0)]

    def other(i):
        d, k = others[i]
        return x_peer(d) * 2 + (core + k) % 2

    def cols(c):
        return pl.ds(pl.multiple_of(c * F, F), F)

    def block(s):
        return pl.ds(pl.multiple_of(s * tokens, tokens), tokens)

    def head_cols(s, h):
        return pl.ds(pl.multiple_of((s * n_heads + h) * hd, hd), hd)

    def head_copy(h, i):
        to = other(i)
        return pltpu.make_async_remote_copy(
            qkv_ref.at[:, :, head_cols(to, h)], heads.at[h, :, block(sp), :], q_s.at[h, i], q_r.at[h, i],
            device_id=(to, ep), device_id_type=MESH,
        )

    def head_local(h):
        return pltpu.make_async_copy(
            qkv_ref.at[:, :, head_cols(sp, h)], heads.at[h, :, block(sp), :], q_l.at[h]
        )

    def weight_copy(i):
        src, dst = ((wg_ref, wg_far), (wu_ref, wu_far), (wd_ref, wd_far))[i]
        return pltpu.make_async_remote_copy(
            src, dst, w_s.at[i], w_r.at[i], device_id=partner, device_id_type=MESH
        )

    def pack_copy(i):
        return pltpu.make_async_remote_copy(
            pack_ref, packs_ref.at[x], k_s.at[i], k_r.at[i], device_id=x_dev(LINE[i]), device_id_type=MESH
        )

    pack_local = pltpu.make_async_copy(pack_ref, packs_ref.at[x], k_l)

    def pair_copy(c):
        return pltpu.make_async_remote_copy(
            pair_out.at[c], pair_in.at[c], p_s.at[c], p_r.at[c], device_id=partner, device_id_type=MESH
        )

    def turn_copy(c, i):
        return pltpu.make_async_remote_copy(
            turn_out.at[c, i], turn_in.at[c, i], t_s.at[c, i], t_r.at[c, i],
            device_id=x_dev((3, 1)[i]), device_id_type=MESH,
        )

    def side_copy(c, i):
        return pltpu.make_async_remote_copy(
            side_out.at[c, i], side_in.at[c, i], s_s.at[c, i], s_r.at[c, i],
            device_id=x_dev((3, 1)[i]), device_id_type=MESH,
        )

    loads = [
        pltpu.make_async_copy(wo_hbm, wo_ref, in_sem.at[0]),
        pltpu.make_async_copy(latent_hbm, latent_ref, in_sem.at[1]),
    ]

    def moe_copy(m):
        at = pl.ds(pl.multiple_of(m * 16, 16), 16)
        return pltpu.make_async_copy(moe_ref.at[at, :], moe_hbm.at[at, :], moe_sem.at[m])

    def res_copy(c):
        return pltpu.make_async_copy(res_ref.at[:, cols(c)], res_hbm.at[:, cols(c)], res_sem.at[c])

    barrier = pltpu.get_barrier_semaphore()
    for i in range(7):
        pl.semaphore_signal(barrier, inc=1, device_id=(other(i), ep), device_id_type=MESH)
    for h in range(n_heads):
        head_local(h).start()
    pack_ref[0:2, :] = (experts_ref[...] * CAP + slots_ref[...]).astype(f32)
    pack_ref[2:4, :] = gates_ref[...]
    pack_ref[4:8, :] = jnp.zeros((4, tokens), f32)
    pack_local.start()
    pl.semaphore_wait(barrier, 7)

    @pl.loop(0, n_heads)
    def _(h):
        for i in range(7):
            head_copy(h, i).start()

    for i in range(3):
        pack_copy(i).start()
    for i in range(3):
        weight_copy(i).start()

    for cp in loads:
        cp.start()
    values[:, hd:] = jnp.ones((window, hd), bf)
    factor = math.log2(math.e) / math.sqrt(hd)
    q_tile = 2 * tokens

    @pl.loop(0, n_heads)
    def _(h):
        head_local(h).wait()
        for i in range(7):
            head_copy(h, i).wait_recv()
        values[:, :hd] = heads[h, 2]

        @pl.loop(0, window // q_tile)
        def _(m):
            at = pl.ds(pl.multiple_of(m * q_tile, q_tile), q_tile)
            scores = lax.dot_general(
                heads[h, 0, at, :], heads[h, 1], (((1,), (1,)), ((), ())), preferred_element_type=f32
            )
            top = jnp.max(scores, axis=1, keepdims=True)
            lifted = jnp.exp2((scores - top) * factor).astype(bf)
            mixed = jnp.dot(lifted, values[...], preferred_element_type=f32)
            out = (mixed[:, :hd] / mixed[:, hd:]).astype(bf)
            to = (block(m), pl.ds(pl.multiple_of(h * hd, hd), hd))
            att[0, to[0], to[1]] = out[:tokens]
            att[1, to[0], to[1]] = out[tokens:]

    for cp in loads:
        cp.wait()

    far_at = (1 - core) * FAR_LATE
    sum_at = 1 + core * (chunks - 1)

    @pl.loop(0, 2 * chunks + 6)
    def _(step):
        @pl.when((step >= far_at) & (step < far_at + chunks))
        def _():
            c = step - far_at
            far = jnp.dot(att[1 - core], wo_ref[:, cols(c)], preferred_element_type=f32)
            pair_out[c] = far.astype(bf)
            pair_copy(c).start()

        @pl.when((step >= sum_at) & (step < sum_at + chunks))
        def _():
            c = step - sum_at
            pair_copy(c).wait_recv()

            def part(b):
                return jnp.dot(
                    att[core, block(b), :], wo_ref[:, cols(c)], preferred_element_type=f32
                ) + pair_in[c, block(b), :].astype(f32)

            over = part(x_peer(2)).astype(bf)
            for i in range(2):
                turn_out[c, i] = over[:, i * H : (i + 1) * H]
                turn_copy(c, i).start()
            side[c, 0] = part(x_peer(3))
            side[c, 1] = part(x_peer(1))
            own[c] = part(x)

        @pl.when((step >= sum_at + 3) & (step < sum_at + chunks + 3))
        def _():
            c = step - sum_at - 3
            for i in range(2):
                turn_copy(c, i).wait_recv()
                near = slice(i * H, (i + 1) * H)
                rest = slice((1 - i) * H, (2 - i) * H)
                side_out[c, i, :, near] = (side[c, i, :, near] + turn_in[c, i].astype(f32)).astype(bf)
                side_out[c, i, :, rest] = side[c, i, :, rest].astype(bf)
                side_copy(c, i).start()

        @pl.when((step >= sum_at + 6) & (step < sum_at + chunks + 6))
        def _():
            c = step - sum_at - 6
            total = own[c]
            for i in range(2):
                side_copy(c, i).wait_recv()
                total = total + side_in[c, i].astype(f32)
            res_ref[:, cols(c)] = latent_ref[:, cols(c)].astype(f32) + mod_ref[0:1, cols(c)] * total
            res_copy(c).start()

    @pl.loop(0, tokens // 16)
    def _(m):
        at = pl.ds(pl.multiple_of(m * 16, 16), 16)
        rows = res_ref[at, :]
        centered = rows - jnp.mean(rows, axis=1, keepdims=True)
        variance = jnp.mean(centered * centered, axis=1, keepdims=True)
        normed = centered * lax.rsqrt(variance + 1e-06)
        moe_ref[at, :] = (normed * (1.0 + mod_ref[2:3, :]) + mod_ref[1:2, :]).astype(bf)
        moe_copy(m).start()

    @pl.loop(0, tokens // 16)
    def _(m):
        moe_copy(m).wait()

    pack_local.wait()
    for i in range(3):
        pack_copy(i).wait()
        weight_copy(i).wait()

    @pl.loop(0, n_heads)
    def _(h):
        for i in range(7):
            head_copy(h, i).wait_send()

    @pl.loop(0, chunks)
    def _(c):
        res_copy(c).wait()
        pair_copy(c).wait_send()
        for i in range(2):
            turn_copy(c, i).wait_send()
            side_copy(c, i).wait_send()


def attention(qkv, latent, out_weight, modulation, routes, weights):
    tokens, width = latent.shape
    chunks = 8
    F = width // chunks
    group = out_weight.shape[0]
    window = 8 * tokens
    bf, f32 = jnp.bfloat16, jnp.float32
    dma = pltpu.SemaphoreType.DMA
    vmem = pl.BlockSpec(memory_space=pltpu.VMEM)
    hbm = pl.BlockSpec(memory_space=pl.ANY)
    outs = pl.pallas_call(
        functools.partial(attention_kernel, chunks),
        out_shape=[
            jax.ShapeDtypeStruct((tokens, width), bf),
            jax.ShapeDtypeStruct((tokens, width), f32),
            jax.ShapeDtypeStruct((4, 8, tokens), f32),
        ]
        + [jax.ShapeDtypeStruct(w.shape, bf) for w in weights],
        in_specs=[hbm] * 3 + [vmem] * 4 + [hbm] * 3,
        out_specs=[hbm] * 6,
        scratch_shapes=[
            pltpu.VMEM((tokens, width), bf),
            pltpu.VMEM((group, width), bf),
            pltpu.VMEM((tokens, width), bf),
            pltpu.VMEM((tokens, width), f32),
            pltpu.VMEM((8, tokens), f32),
            pltpu.VMEM((group // HD, 3, window, HD), bf),
            pltpu.VMEM((window, 2 * HD), bf),
            pltpu.VMEM((2, window // 2, group), bf),
            pltpu.VMEM((chunks, window // 2, F), bf),
            pltpu.VMEM((chunks, window // 2, F), bf),
            pltpu.VMEM((chunks, 2, tokens, F // 2), bf),
            pltpu.VMEM((chunks, 2, tokens, F // 2), bf),
            pltpu.VMEM((chunks, 2, tokens, F), f32),
            pltpu.VMEM((chunks, 2, tokens, F), bf),
            pltpu.VMEM((chunks, 2, tokens, F), bf),
            pltpu.VMEM((chunks, tokens, F), f32),
            dma((4, 7)), dma((4, 7)), dma((4,)),
            dma((chunks,)), dma((chunks,)),
            dma((chunks, 2)), dma((chunks, 2)),
            dma((chunks, 2)), dma((chunks, 2)),
            dma((3,)), dma((3,)), dma((3,)), dma((3,)), dma,
            dma((2,)), dma((tokens // 16,)), dma((chunks,)),
        ],
        compiler_params=pltpu.CompilerParams(
            collective_id=1, has_side_effects=True, vmem_limit_bytes=60 * 1024 * 1024
        ),
        cost_estimate=pl.CostEstimate(flops=6_500_000_000, bytes_accessed=40_000_000, transcendentals=4_200_000),
        name="attention",
    )(qkv, latent, out_weight, modulation, *routes, *weights)
    return outs[0], outs[1], outs[2], outs[3:]


def expert_kernel(
    chunks,
    moe_ref, res_hbm, mod_ref, packs_ref, wg_own, wg_far, wu_own, wu_far, wd_own, wd_far,
    out_ref,
    tok, send, recv, back, mate, turn_in, side_in, acc_g, acc_u, act, wg, wu, wd, spread, merge, part_ref, res_ref,
    a_s, a_r, f_s, f_r, d_s, d_r, r_s, r_r, m_s, m_r, n_s, n_r, t_s, t_r, s_s, s_r, w_sem, wd_sem, own_sem, res_sem,
):
    sp, ep = lax.axis_index("sp"), lax.axis_index("ep")
    x, core = sp // 2, sp % 2
    z, y = ep // 4, ep % 4
    mine = x % 2
    F = tok.shape[3]
    H = F // 2
    half = wg_own.shape[1]
    rows = send.shape[2]
    tokens = tok.shape[2]
    f32, bf = jnp.float32, jnp.bfloat16

    def x_dev(d):
        return (((x + d) % 4) * 2 + core, ep)

    mate_dev = ((x + 1 - 2 * mine) * 2 + core, ep)

    def offset(m, i):
        return i // 2, (2 * (i % 2) + (i // 2) % 2 + m) % 4

    def plane_dev(m, i, sign):
        dz, dy = offset(m, i)
        return (sp, ((z + sign * dz + 4) % 4) * 4 + (y + sign * dy + 4) % 4)

    seats = [(q // 8, q % 8) for q in range(1, 16)]
    order = [next(q for q in seats if offset(*q) == o) for o in PLANE]

    barrier = pltpu.get_barrier_semaphore()
    for d in LINE:
        pl.semaphore_signal(barrier, inc=1, device_id=x_dev(d), device_id_type=MESH)
    for m, i in order:
        pl.semaphore_signal(barrier, inc=1, device_id=plane_dev(m, i, 1), device_id_type=MESH)

    def shared(c):
        return (c % 2 == 1) & (c < 2 * SHARED)

    def cols(c):
        return pl.ds(pl.multiple_of(c * F, F), F)

    def seat(i):
        return pl.ds(i * BLOCK_SLOTS, BLOCK_SLOTS)

    def w_copies(k):
        s = k % W_SLOTS
        return [
            pltpu.make_async_copy(src.at[cols(k), :], dst.at[s, :, pl.ds(at, half)], w_sem.at[s, i])
            for i, (src, dst, at) in enumerate(
                ((wg_own, wg, 0), (wg_far, wg, half), (wu_own, wu, 0), (wu_far, wu, half))
            )
        ]

    def wd_copies(k):
        s = k % D_SLOTS
        return [
            pltpu.make_async_copy(src.at[:, cols(k)], wd.at[s, pl.ds(at, half), :], wd_sem.at[s, i])
            for i, (src, at) in enumerate(((wd_own, 0), (wd_far, half)))
        ]

    def own_copy(c):
        return pltpu.make_async_copy(moe_ref.at[:, cols(c)], tok.at[c, x], own_sem.at[c])

    res_copy = pltpu.make_async_copy(res_hbm, res_ref, res_sem)

    def near_copy(c, i):
        return pltpu.make_async_remote_copy(
            moe_ref.at[:, cols(c)], tok.at[c, x], a_s.at[c, i], a_r.at[c, i],
            device_id=x_dev((1, 3)[i]), device_id_type=MESH,
        )

    def pass_copy(c, i):
        block = tok.at[c, (x + (1, 3)[i]) % 4, :, pl.ds(i * H, H)]
        return pltpu.make_async_remote_copy(
            block, block, f_s.at[c, i], f_r.at[c, i], device_id=x_dev((3, 1)[i]), device_id_type=MESH
        )

    def seat_copy(c, m, i, dst, s_sem, r_sem, sign):
        return pltpu.make_async_remote_copy(
            send.at[c, m, seat(i)], dst.at[c, m, seat(i)], s_sem.at[c, m * 8 + i], r_sem.at[c, m * 8 + i],
            device_id=plane_dev(m, i, sign), device_id_type=MESH,
        )

    def seat_copies(c, way, act_on):
        args = (recv, d_s, d_r, 1) if way == 0 else (back, r_s, r_r, -1)

        @pl.when(shared(c))
        def _():
            for i in SET_ORDER:
                act_on(seat_copy(c, mine, i, *args))

            @pl.when(mine == 1)
            def _():
                act_on(seat_copy(c, mine, 0, *args))

        @pl.when(jnp.logical_not(shared(c)))
        def _():
            for m, i in order:
                act_on(seat_copy(c, m, i, *args))

    def start(copy):
        copy.start()

    def wait_recv(copy):
        copy.wait_recv()

    def wait_send(copy):
        copy.wait_send()

    def mate_rows(c):
        return pltpu.make_async_remote_copy(
            recv.at[c, mine], recv.at[c, mine], m_s.at[c], m_r.at[c], device_id=mate_dev, device_id_type=MESH
        )

    def mate_sums(c):
        return pltpu.make_async_remote_copy(
            send.at[c, 1 - mine], mate.at[c // 2], n_s.at[c], n_r.at[c], device_id=mate_dev, device_id_type=MESH
        )

    def turn_copy(c, i):
        return pltpu.make_async_remote_copy(
            tok.at[c, 0, :, pl.ds(i * H, H)], turn_in.at[c, i], t_s.at[c, i], t_r.at[c, i],
            device_id=x_dev((3, 1)[i]), device_id_type=MESH,
        )

    def side_copy(c, i):
        return pltpu.make_async_remote_copy(
            tok.at[c, 1 + i], side_in.at[c, i], s_s.at[c, i], s_r.at[c, i],
            device_id=x_dev((3, 1)[i]), device_id_type=MESH,
        )

    pl.semaphore_wait(barrier, len(LINE) + len(PLANE))

    @pl.loop(0, 2)
    def _(c):
        for i in range(2):
            near_copy(c, i).start()

    @pl.loop(0, chunks)
    def _(c):
        own_copy(c).start()

    for k in range(W_SLOTS):
        for cp in w_copies(k):
            cp.start()
    for k in range(D_SLOTS):
        for cp in wd_copies(k):
            cp.start()
    res_copy.start()

    row = lax.broadcasted_iota(jnp.int32, (rows, 1), 0)
    place, rest = row // BLOCK_SLOTS, row % BLOCK_SLOTS
    block, slot = rest // CAP, rest % CAP
    for m in range(2):
        dz, dy = offset(m, place)
        pair = ((z + dz) % 4) * 4 + (y + dy) % 4
        wanted = (2 * pair + x // 2) * CAP + slot
        for b in range(4):
            at = slice(b * tokens, (b + 1) * tokens)
            key = jnp.where(block == b, wanted, -1).astype(f32)
            first = packs_ref[b, 0:1, :] == key
            second = packs_ref[b, 1:2, :] == key
            spread[m, :, at] = jnp.where(first | second, 1.0, 0.0).astype(bf)
            weight = jnp.where(first, packs_ref[b, 2:3, :], 0.0) + jnp.where(second, packs_ref[b, 3:4, :], 0.0)
            merge[m, at, :] = weight.T.astype(bf)

    acc_g[...] = jnp.zeros_like(acc_g)
    acc_u[...] = jnp.zeros_like(acc_u)

    def pass_on(c):
        for i in range(2):
            near_copy(c, 1 - i).wait_recv()
            pass_copy(c, i).start()

        @pl.when(c + 2 < chunks)
        def _():
            for i in range(2):
                near_copy(c + 2, i).start()

    pass_on(0)

    @pl.loop(0, chunks + 2)
    def _(step):
        @pl.when(step + 1 < chunks)
        def _():
            pass_on(step + 1)

        @pl.when(step < chunks)
        def _():
            c = step
            own_copy(c).wait()
            for i in range(2):
                pass_copy(c, i).wait_recv()
            lines = tok[c].reshape(4 * tokens, F)

            @pl.loop(0, 2)
            def _(m):
                @pl.when(jnp.logical_not(shared(c)) | (m == mine))
                def _():
                    send[c, m] = jnp.dot(spread[m], lines, preferred_element_type=f32).astype(bf)

            seat_copies(c, 0, start)

            @pl.when(jnp.logical_not(shared(c)) | (mine == 0))
            def _():
                recv[c, 0, seat(0)] = send[c, 0, seat(0)]

        @pl.when(step >= 3)
        def _():
            k = step - 3
            s = k % W_SLOTS
            for cp in w_copies(k):
                cp.wait()

            @pl.when(shared(k))
            def _():
                mate_rows(k).wait_recv()

            @pl.when(jnp.logical_not(shared(k)))
            def _():
                for m, i in order:
                    seat_copy(k, m, i, recv, d_s, d_r, 1).wait_recv()

            @pl.loop(0, 2)
            def _(m):
                lines = recv[k, m]
                acc_g[m] += jnp.dot(lines, wg[s], preferred_element_type=f32)
                acc_u[m] += jnp.dot(lines, wu[s], preferred_element_type=f32)

            @pl.when(k + W_SLOTS < chunks)
            def _():
                for cp in w_copies(k + W_SLOTS):
                    cp.start()

        @pl.when((step >= 2) & shared(step - 2))
        def _():
            k = step - 2
            for i in SET_ORDER:
                seat_copy(k, mine, i, recv, d_s, d_r, 1).wait_recv()

            @pl.when(mine == 1)
            def _():
                seat_copy(k, mine, 0, recv, d_s, d_r, 1).wait_recv()

            mate_rows(k).start()

    last = chunks - 1
    for cp in w_copies(last) + wd_copies(0):
        cp.wait()
    seat_copies(last, 0, wait_recv)
    seat_copies(0, 0, wait_send)
    res_copy.wait()

    @pl.loop(0, 2)
    def _(m):
        lines = recv[last, m]
        acc_g[m] += jnp.dot(lines, wg[last % W_SLOTS], preferred_element_type=f32)
        acc_u[m] += jnp.dot(lines, wu[last % W_SLOTS], preferred_element_type=f32)

        @pl.loop(0, rows // 64)
        def _(t):
            at = pl.ds(pl.multiple_of(t * 64, 64), 64)
            g = acc_g[m, at, :]
            act[m, at, :] = (g / (1.0 + jnp.exp(-g)) * acc_u[m, at, :]).astype(bf)

        send[0, m] = jnp.dot(act[m], wd[0], preferred_element_type=f32).astype(bf)
        for i in SET_ORDER:
            seat_copy(0, m, i, back, r_s, r_r, -1).start()

        @pl.when(m == 1)
        def _():
            seat_copy(0, m, 0, back, r_s, r_r, -1).start()

        @pl.when(m == 0)
        def _():
            back[0, 0, seat(0)] = send[0, 0, seat(0)]

    def part(k, b):
        at = pl.ds(pl.multiple_of(b * tokens, tokens), tokens)
        part_ref[...] = jnp.dot(merge[mine, at, :], back[k, mine], preferred_element_type=f32)

        @pl.when(jnp.logical_not(shared(k)))
        def _():
            part_ref[...] += jnp.dot(merge[1 - mine, at, :], back[k, 1 - mine], preferred_element_type=f32)

        return part_ref[...]

    @pl.loop(0, chunks + 6)
    def _(step):
        @pl.when((step >= 1) & (step < chunks))
        def _():
            c = step
            s = c % D_SLOTS
            for cp in wd_copies(c):
                cp.wait()
            seat_copies(c, 0, wait_send)

            @pl.loop(0, 2)
            def _(m):
                @pl.when(jnp.logical_not(shared(c)) | (m != mine))
                def _():
                    send[c, m] = jnp.dot(act[m], wd[s], preferred_element_type=f32).astype(bf)

            @pl.when(shared(c))
            def _():
                mate_sums(c).start()

            @pl.when(jnp.logical_not(shared(c)))
            def _():
                for m, i in order:
                    seat_copy(c, m, i, back, r_s, r_r, -1).start()
                back[c, 0, seat(0)] = send[c, 0, seat(0)]

        @pl.when((step >= 1) & (step < chunks + 1))
        def _():
            k = step - 1

            @pl.when(shared(k))
            def _():
                mate_sums(k).wait_recv()
                both = jnp.dot(act[mine], wd[k % D_SLOTS], preferred_element_type=f32) + mate[k // 2].astype(f32)
                send[k, mine] = both.astype(bf)
                for i in SET_ORDER:
                    seat_copy(k, mine, i, back, r_s, r_r, -1).start()

                @pl.when(mine == 1)
                def _():
                    seat_copy(k, mine, 0, back, r_s, r_r, -1).start()

                @pl.when(mine == 0)
                def _():
                    back[k, 0, seat(0)] = send[k, 0, seat(0)]

            @pl.when(k + D_SLOTS < chunks)
            def _():
                for cp in wd_copies(k + D_SLOTS):
                    cp.start()

        @pl.when((step >= 3) & (step < chunks + 3))
        def _():
            k = step - 3
            seat_copies(k, 1, wait_recv)
            for i in range(2):
                pass_copy(k, i).wait_send()
            tok[k, 0] = part(k, (x + 2) % 4).astype(bf)
            for i in range(2):
                turn_copy(k, i).start()

        @pl.when((step >= 4) & (step < chunks + 4))
        def _():
            k = step - 4
            for i in range(2):
                near = slice(i * H, (i + 1) * H)
                rest = slice((1 - i) * H, (2 - i) * H)
                side = part(k, (x + (3, 1)[i]) % 4)
                turn_copy(k, i).wait_recv()
                tok[k, 1 + i, :, near] = (side[:, near] + turn_in[k, i].astype(f32)).astype(bf)
                tok[k, 1 + i, :, rest] = side[:, rest].astype(bf)
                side_copy(k, i).start()

        @pl.when(step >= 6)
        def _():
            k = step - 6
            total = part(k, x)
            for i in range(2):
                side_copy(k, i).wait_recv()
                total = total + side_in[k, i].astype(f32)
            out_ref[:, cols(k)] = (res_ref[:, cols(k)] + mod_ref[3:4, cols(k)] * total).astype(out_ref.dtype)

    @pl.loop(0, chunks)
    def _(c):
        for i in range(2):
            near_copy(c, i).wait_send()
            turn_copy(c, i).wait_send()
            side_copy(c, i).wait_send()
        seat_copies(c, 1, wait_send)

        @pl.when(shared(c))
        def _():
            mate_rows(c).wait_send()
            mate_sums(c).wait_send()


def experts(moe_in, residual, modulation, packs, weights):
    tokens, width = moe_in.shape
    chunks = 8
    F = width // chunks
    rows = 8 * BLOCK_SLOTS
    hidden = 2 * weights[0].shape[1]
    bf, f32 = jnp.bfloat16, jnp.float32
    dma = pltpu.SemaphoreType.DMA
    vmem = pl.BlockSpec(memory_space=pltpu.VMEM)
    hbm = pl.BlockSpec(memory_space=pl.ANY)
    return pl.pallas_call(
        functools.partial(expert_kernel, chunks),
        out_shape=jax.ShapeDtypeStruct((tokens, width), bf),
        in_specs=[hbm] * 2 + [vmem] * 2 + [hbm] * 6,
        out_specs=vmem,
        scratch_shapes=[
            pltpu.VMEM((chunks, 4, tokens, F), bf),
            pltpu.VMEM((chunks, 2, rows, F), bf),
            pltpu.VMEM((chunks, 2, rows, F), bf),
            pltpu.VMEM((chunks, 2, rows, F), bf),
            pltpu.VMEM((SHARED, rows, F), bf),
            pltpu.VMEM((chunks, 2, tokens, F // 2), bf),
            pltpu.VMEM((chunks, 2, tokens, F), bf),
            pltpu.VMEM((2, rows, hidden), f32),
            pltpu.VMEM((2, rows, hidden), f32),
            pltpu.VMEM((2, rows, hidden), bf),
            pltpu.VMEM((W_SLOTS, F, hidden), bf),
            pltpu.VMEM((W_SLOTS, F, hidden), bf),
            pltpu.VMEM((D_SLOTS, hidden, F), bf),
            pltpu.VMEM((2, rows, 4 * tokens), bf),
            pltpu.VMEM((2, 4 * tokens, rows), bf),
            pltpu.VMEM((tokens, F), f32),
            pltpu.VMEM((tokens, width), f32),
        ]
        + [dma((chunks, 2))] * 4
        + [dma((chunks, 16))] * 4
        + [dma((chunks,))] * 4
        + [dma((chunks, 2))] * 4
        + [dma((W_SLOTS, 4)), dma((D_SLOTS, 2)), dma((chunks,)), dma],
        compiler_params=pltpu.CompilerParams(
            collective_id=0, has_side_effects=True, vmem_limit_bytes=62 * 1024 * 1024
        ),
        cost_estimate=pl.CostEstimate(flops=26_000_000_000, bytes_accessed=40_000_000, transcendentals=800_000),
        name="experts",
    )(moe_in, residual, modulation, packs, *weights)


def local(
    latent,
    attention_in,
    out_weight,
    modulation,
    route_experts,
    route_slots,
    route_gates,
    gate_weight,
    up_weight,
    down_weight,
):
    weights = [gate_weight[0], up_weight[0], down_weight[0]]
    routes = [route_experts[0].T, route_slots[0].T, route_gates[0].T]
    qkv = jnp.transpose(attention_in[0], (1, 0, 2))
    moe_in, residual, packs, far = attention(qkv, latent[0], out_weight, modulation, routes, weights)
    both = [w for pair in zip(weights, far) for w in pair]
    return experts(moe_in, residual, modulation, packs, both)[None]


def solution(mesh):
    return jax.shard_map(
        local,
        mesh=mesh,
        in_specs=(
            P("ep", "sp", None),
            P("ep", "sp", None, None),
            P("sp", None),
            P(),
            P("ep", "sp", None),
            P("ep", "sp", None),
            P("ep", "sp", None),
            P("ep", None, "sp"),
            P("ep", None, "sp"),
            P("ep", "sp", None),
        ),
        out_specs=P("ep", "sp", None),
        check_vma=False,
    )
```

```python
import functools
import math

import jax
import jax.numpy as jnp
from jax import lax
from jax.experimental import pallas as pl
from jax.experimental.pallas import tpu as pltpu
from jax.sharding import PartitionSpec as P

HD = 128
MESH = pl.DeviceIdType.MESH

PLANE = (
    (2, 2), (1, 0), (0, 1), (3, 0), (0, 3), (2, 1), (1, 2), (2, 3), (3, 2),
    (1, 1), (3, 3), (2, 0), (0, 2), (1, 3), (3, 1),
)
LINE = (1, 3, 2)
CAP = 12
BLOCK_SLOTS = 4 * CAP
FAR_LATE = 8
W_SLOTS = 3
D_SLOTS = 5
SHARED = 3
SET_ORDER = (1, 2, 4, 7, 3, 6, 5)


def attention_kernel(
    chunks,
    qkv_ref, latent_hbm, wo_hbm, mod_ref, experts_ref, slots_ref, gates_ref, wg_ref, wu_ref, wd_ref,
    moe_hbm, res_hbm, packs_ref, wg_far, wu_far, wd_far,
    latent_ref, wo_ref, moe_ref, res_ref, pack_ref, heads, values, att, pair_out, pair_in, turn_out, turn_in, side, side_out, side_in, own,
    q_s, q_r, q_l, p_s, p_r, t_s, t_r, s_s, s_r, w_s, w_r, k_s, k_r, k_l, in_sem, moe_sem, res_sem,
):
    sp, ep = lax.axis_index("sp"), lax.axis_index("ep")
    x, core = sp // 2, sp % 2
    n_heads, _, window, hd = heads.shape
    tokens = window // 8
    F = wo_ref.shape[1] // chunks
    H = F // 2
    f32, bf = jnp.float32, jnp.bfloat16

    def x_peer(d):
        return (x + d) % 4

    def x_dev(d):
        return (x_peer(d) * 2 + core, ep)

    partner = (x * 2 + 1 - core, ep)
    others = [(d, k) for d in (2, 1, 3, 0) for k in (0, 1) if (d, k) != (0, 0)]

    def other(i):
        d, k = others[i]
        return x_peer(d) * 2 + (core + k) % 2

    def cols(c):
        return pl.ds(pl.multiple_of(c * F, F), F)

    def block(s):
        return pl.ds(pl.multiple_of(s * tokens, tokens), tokens)

    def head_cols(s, h):
        return pl.ds(pl.multiple_of((s * n_heads + h) * hd, hd), hd)

    def head_copy(h, i):
        to = other(i)
        return pltpu.make_async_remote_copy(
            qkv_ref.at[:, :, head_cols(to, h)], heads.at[h, :, block(sp), :], q_s.at[h, i], q_r.at[h, i],
            device_id=(to, ep), device_id_type=MESH,
        )

    def head_local(h):
        return pltpu.make_async_copy(
            qkv_ref.at[:, :, head_cols(sp, h)], heads.at[h, :, block(sp), :], q_l.at[h]
        )

    def weight_copy(i):
        src, dst = ((wg_ref, wg_far), (wu_ref, wu_far), (wd_ref, wd_far))[i]
        return pltpu.make_async_remote_copy(
            src, dst, w_s.at[i], w_r.at[i], device_id=partner, device_id_type=MESH
        )

    def pack_copy(i):
        return pltpu.make_async_remote_copy(
            pack_ref, packs_ref.at[x], k_s.at[i], k_r.at[i], device_id=x_dev(LINE[i]), device_id_type=MESH
        )

    pack_local = pltpu.make_async_copy(pack_ref, packs_ref.at[x], k_l)

    def pair_copy(c):
        return pltpu.make_async_remote_copy(
            pair_out.at[c], pair_in.at[c], p_s.at[c], p_r.at[c], device_id=partner, device_id_type=MESH
        )

    def turn_copy(c, i):
        return pltpu.make_async_remote_copy(
            turn_out.at[c, i], turn_in.at[c, i], t_s.at[c, i], t_r.at[c, i],
            device_id=x_dev((3, 1)[i]), device_id_type=MESH,
        )

    def side_copy(c, i):
        return pltpu.make_async_remote_copy(
            side_out.at[c, i], side_in.at[c, i], s_s.at[c, i], s_r.at[c, i],
            device_id=x_dev((3, 1)[i]), device_id_type=MESH,
        )

    loads = [
        pltpu.make_async_copy(wo_hbm, wo_ref, in_sem.at[0]),
        pltpu.make_async_copy(latent_hbm, latent_ref, in_sem.at[1]),
    ]

    def moe_copy(m):
        at = pl.ds(pl.multiple_of(m * 16, 16), 16)
        return pltpu.make_async_copy(moe_ref.at[at, :], moe_hbm.at[at, :], moe_sem.at[m])

    def res_copy(c):
        return pltpu.make_async_copy(res_ref.at[:, cols(c)], res_hbm.at[:, cols(c)], res_sem.at[c])

    barrier = pltpu.get_barrier_semaphore()
    for i in range(7):
        pl.semaphore_signal(barrier, inc=1, device_id=(other(i), ep), device_id_type=MESH)
    for h in range(n_heads):
        head_local(h).start()
    pack_ref[0:2, :] = (experts_ref[...] * CAP + slots_ref[...]).astype(f32)
    pack_ref[2:4, :] = gates_ref[...]
    pack_ref[4:8, :] = jnp.zeros((4, tokens), f32)
    pack_local.start()
    pl.semaphore_wait(barrier, 7)

    @pl.loop(0, n_heads)
    def _(h):
        for i in range(7):
            head_copy(h, i).start()

    for i in range(3):
        pack_copy(i).start()
    for i in range(3):
        weight_copy(i).start()

    for cp in loads:
        cp.start()
    values[:, hd:] = jnp.ones((window, hd), bf)
    factor = math.log2(math.e) / math.sqrt(hd)
    q_tile = 2 * tokens

    @pl.loop(0, n_heads)
    def _(h):
        head_local(h).wait()
        for i in range(7):
            head_copy(h, i).wait_recv()
        values[:, :hd] = heads[h, 2]

        @pl.loop(0, window // q_tile)
        def _(m):
            at = pl.ds(pl.multiple_of(m * q_tile, q_tile), q_tile)
            scores = lax.dot_general(
                heads[h, 0, at, :], heads[h, 1], (((1,), (1,)), ((), ())), preferred_element_type=f32
            )
            top = jnp.max(scores, axis=1, keepdims=True)
            lifted = jnp.exp2((scores - top) * factor).astype(bf)
            mixed = jnp.dot(lifted, values[...], preferred_element_type=f32)
            out = (mixed[:, :hd] / mixed[:, hd:]).astype(bf)
            to = (block(m), pl.ds(pl.multiple_of(h * hd, hd), hd))
            att[0, to[0], to[1]] = out[:tokens]
            att[1, to[0], to[1]] = out[tokens:]

    for cp in loads:
        cp.wait()

    far_at = (1 - core) * FAR_LATE
    sum_at = 1 + core * (chunks - 1)

    @pl.loop(0, 2 * chunks + 6)
    def _(step):
        @pl.when((step >= far_at) & (step < far_at + chunks))
        def _():
            c = step - far_at
            far = jnp.dot(att[1 - core], wo_ref[:, cols(c)], preferred_element_type=f32)
            pair_out[c] = far.astype(bf)
            pair_copy(c).start()

        @pl.when((step >= sum_at) & (step < sum_at + chunks))
        def _():
            c = step - sum_at
            pair_copy(c).wait_recv()

            def part(b):
                return jnp.dot(
                    att[core, block(b), :], wo_ref[:, cols(c)], preferred_element_type=f32
                ) + pair_in[c, block(b), :].astype(f32)

            over = part(x_peer(2)).astype(bf)
            for i in range(2):
                turn_out[c, i] = over[:, i * H : (i + 1) * H]
                turn_copy(c, i).start()
            side[c, 0] = part(x_peer(3))
            side[c, 1] = part(x_peer(1))
            own[c] = part(x)

        @pl.when((step >= sum_at + 3) & (step < sum_at + chunks + 3))
        def _():
            c = step - sum_at - 3
            for i in range(2):
                turn_copy(c, i).wait_recv()
                near = slice(i * H, (i + 1) * H)
                rest = slice((1 - i) * H, (2 - i) * H)
                side_out[c, i, :, near] = (side[c, i, :, near] + turn_in[c, i].astype(f32)).astype(bf)
                side_out[c, i, :, rest] = side[c, i, :, rest].astype(bf)
                side_copy(c, i).start()

        @pl.when((step >= sum_at + 6) & (step < sum_at + chunks + 6))
        def _():
            c = step - sum_at - 6
            total = own[c]
            for i in range(2):
                side_copy(c, i).wait_recv()
                total = total + side_in[c, i].astype(f32)
            res_ref[:, cols(c)] = latent_ref[:, cols(c)].astype(f32) + mod_ref[0:1, cols(c)] * total
            res_copy(c).start()

    @pl.loop(0, tokens // 16)
    def _(m):
        at = pl.ds(pl.multiple_of(m * 16, 16), 16)
        rows = res_ref[at, :]
        centered = rows - jnp.mean(rows, axis=1, keepdims=True)
        variance = jnp.mean(centered * centered, axis=1, keepdims=True)
        normed = centered * lax.rsqrt(variance + 1e-06)
        moe_ref[at, :] = (normed * (1.0 + mod_ref[2:3, :]) + mod_ref[1:2, :]).astype(bf)
        moe_copy(m).start()

    @pl.loop(0, tokens // 16)
    def _(m):
        moe_copy(m).wait()

    pack_local.wait()
    for i in range(3):
        pack_copy(i).wait()
        weight_copy(i).wait()

    @pl.loop(0, n_heads)
    def _(h):
        for i in range(7):
            head_copy(h, i).wait_send()

    @pl.loop(0, chunks)
    def _(c):
        res_copy(c).wait()
        pair_copy(c).wait_send()
        for i in range(2):
            turn_copy(c, i).wait_send()
            side_copy(c, i).wait_send()


def attention(qkv, latent, out_weight, modulation, routes, weights):
    tokens, width = latent.shape
    chunks = 8
    F = width // chunks
    group = out_weight.shape[0]
    window = 8 * tokens
    bf, f32 = jnp.bfloat16, jnp.float32
    dma = pltpu.SemaphoreType.DMA
    vmem = pl.BlockSpec(memory_space=pltpu.VMEM)
    hbm = pl.BlockSpec(memory_space=pl.ANY)
    outs = pl.pallas_call(
        functools.partial(attention_kernel, chunks),
        out_shape=[
            jax.ShapeDtypeStruct((tokens, width), bf),
            jax.ShapeDtypeStruct((tokens, width), f32),
            jax.ShapeDtypeStruct((4, 8, tokens), f32),
        ]
        + [jax.ShapeDtypeStruct(w.shape, bf) for w in weights],
        in_specs=[hbm] * 3 + [vmem] * 4 + [hbm] * 3,
        out_specs=[hbm] * 6,
        scratch_shapes=[
            pltpu.VMEM((tokens, width), bf),
            pltpu.VMEM((group, width), bf),
            pltpu.VMEM((tokens, width), bf),
            pltpu.VMEM((tokens, width), f32),
            pltpu.VMEM((8, tokens), f32),
            pltpu.VMEM((group // HD, 3, window, HD), bf),
            pltpu.VMEM((window, 2 * HD), bf),
            pltpu.VMEM((2, window // 2, group), bf),
            pltpu.VMEM((chunks, window // 2, F), bf),
            pltpu.VMEM((chunks, window // 2, F), bf),
            pltpu.VMEM((chunks, 2, tokens, F // 2), bf),
            pltpu.VMEM((chunks, 2, tokens, F // 2), bf),
            pltpu.VMEM((chunks, 2, tokens, F), f32),
            pltpu.VMEM((chunks, 2, tokens, F), bf),
            pltpu.VMEM((chunks, 2, tokens, F), bf),
            pltpu.VMEM((chunks, tokens, F), f32),
            dma((4, 7)), dma((4, 7)), dma((4,)),
            dma((chunks,)), dma((chunks,)),
            dma((chunks, 2)), dma((chunks, 2)),
            dma((chunks, 2)), dma((chunks, 2)),
            dma((3,)), dma((3,)), dma((3,)), dma((3,)), dma,
            dma((2,)), dma((tokens // 16,)), dma((chunks,)),
        ],
        compiler_params=pltpu.CompilerParams(
            collective_id=1, has_side_effects=True, vmem_limit_bytes=60 * 1024 * 1024
        ),
        cost_estimate=pl.CostEstimate(flops=6_500_000_000, bytes_accessed=40_000_000, transcendentals=4_200_000),
        name="attention",
    )(qkv, latent, out_weight, modulation, *routes, *weights)
    return outs[0], outs[1], outs[2], outs[3:]


def expert_kernel(
    chunks,
    moe_ref, res_hbm, mod_ref, packs_ref, wg_own, wg_far, wu_own, wu_far, wd_own, wd_far,
    out_ref,
    tok, send, recv, back, mate, turn_in, side_in, acc_g, acc_u, act, wg, wu, wd, spread, merge, part_ref, res_ref,
    a_s, a_r, f_s, f_r, d_s, d_r, r_s, r_r, m_s, m_r, n_s, n_r, t_s, t_r, s_s, s_r, w_sem, wd_sem, own_sem, res_sem,
):
    sp, ep = lax.axis_index("sp"), lax.axis_index("ep")
    x, core = sp // 2, sp % 2
    z, y = ep // 4, ep % 4
    mine = x % 2
    F = tok.shape[3]
    H = F // 2
    half = wg_own.shape[1]
    rows = send.shape[2]
    tokens = tok.shape[2]
    f32, bf = jnp.float32, jnp.bfloat16

    def x_dev(d):
        return (((x + d) % 4) * 2 + core, ep)

    mate_dev = ((x + 1 - 2 * mine) * 2 + core, ep)

    def offset(m, i):
        return i // 2, (2 * (i % 2) + (i // 2) % 2 + m) % 4

    def plane_dev(m, i, sign):
        dz, dy = offset(m, i)
        return (sp, ((z + sign * dz + 4) % 4) * 4 + (y + sign * dy + 4) % 4)

    seats = [(q // 8, q % 8) for q in range(1, 16)]
    order = [next(q for q in seats if offset(*q) == o) for o in PLANE]
    turned = [next(q for q in seats if offset(*q) == ((4 - o[0]) % 4, (4 - o[1]) % 4)) for o in PLANE]
    by_core = [(m, jnp.where(core == 0, i, j)) for (m, i), (_, j) in zip(order, turned)]

    barrier = pltpu.get_barrier_semaphore()
    for d in LINE:
        pl.semaphore_signal(barrier, inc=1, device_id=x_dev(d), device_id_type=MESH)
    for m, i in order:
        pl.semaphore_signal(barrier, inc=1, device_id=plane_dev(m, i, 1), device_id_type=MESH)

    def shared(c):
        return (c % 2 == 1) & (c < 2 * SHARED)

    def cols(c):
        return pl.ds(pl.multiple_of(c * F, F), F)

    def seat(i):
        return pl.ds(pl.multiple_of(i * BLOCK_SLOTS, 16), BLOCK_SLOTS)

    def w_copies(k):
        s = k % W_SLOTS
        return [
            pltpu.make_async_copy(src.at[cols(k), :], dst.at[s, :, pl.ds(at, half)], w_sem.at[s, i])
            for i, (src, dst, at) in enumerate(
                ((wg_own, wg, 0), (wg_far, wg, half), (wu_own, wu, 0), (wu_far, wu, half))
            )
        ]

    def wd_copies(k):
        s = k % D_SLOTS
        return [
            pltpu.make_async_copy(src.at[:, cols(k)], wd.at[s, pl.ds(at, half), :], wd_sem.at[s, i])
            for i, (src, at) in enumerate(((wd_own, 0), (wd_far, half)))
        ]

    def own_copy(c):
        return pltpu.make_async_copy(moe_ref.at[:, cols(c)], tok.at[c, x], own_sem.at[c])

    res_copy = pltpu.make_async_copy(res_hbm, res_ref, res_sem)

    def near_copy(c, i):
        return pltpu.make_async_remote_copy(
            moe_ref.at[:, cols(c)], tok.at[c, x], a_s.at[c, i], a_r.at[c, i],
            device_id=x_dev((1, 3)[i]), device_id_type=MESH,
        )

    def pass_copy(c, i):
        block = tok.at[c, (x + (1, 3)[i]) % 4, :, pl.ds(i * H, H)]
        return pltpu.make_async_remote_copy(
            block, block, f_s.at[c, i], f_r.at[c, i], device_id=x_dev((3, 1)[i]), device_id_type=MESH
        )

    def seat_copy(c, m, i, dst, s_sem, r_sem, sign):
        return pltpu.make_async_remote_copy(
            send.at[c, m, seat(i)], dst.at[c, m, seat(i)], s_sem.at[c, m * 8 + i], r_sem.at[c, m * 8 + i],
            device_id=plane_dev(m, i, sign), device_id_type=MESH,
        )

    def seat_copies(c, way, act_on):
        args = (recv, d_s, d_r, 1) if way == 0 else (back, r_s, r_r, -1)

        @pl.when(shared(c))
        def _():
            for i in SET_ORDER:
                act_on(seat_copy(c, mine, i, *args))

            @pl.when(mine == 1)
            def _():
                act_on(seat_copy(c, mine, 0, *args))

        @pl.when(jnp.logical_not(shared(c)))
        def _():
            for m, i in by_core:
                act_on(seat_copy(c, m, i, *args))

    def start(copy):
        copy.start()

    def wait_recv(copy):
        copy.wait_recv()

    def wait_send(copy):
        copy.wait_send()

    def mate_rows(c):
        return pltpu.make_async_remote_copy(
            recv.at[c, mine], recv.at[c, mine], m_s.at[c], m_r.at[c], device_id=mate_dev, device_id_type=MESH
        )

    def mate_sums(c):
        return pltpu.make_async_remote_copy(
            send.at[c, 1 - mine], mate.at[c // 2], n_s.at[c], n_r.at[c], device_id=mate_dev, device_id_type=MESH
        )

    def turn_copy(c, i):
        return pltpu.make_async_remote_copy(
            tok.at[c, 0, :, pl.ds(i * H, H)], turn_in.at[c, i], t_s.at[c, i], t_r.at[c, i],
            device_id=x_dev((3, 1)[i]), device_id_type=MESH,
        )

    def side_copy(c, i):
        return pltpu.make_async_remote_copy(
            tok.at[c, 1 + i], side_in.at[c, i], s_s.at[c, i], s_r.at[c, i],
            device_id=x_dev((3, 1)[i]), device_id_type=MESH,
        )

    pl.semaphore_wait(barrier, len(LINE) + len(PLANE))

    @pl.loop(0, 2)
    def _(c):
        for i in range(2):
            near_copy(c, i).start()

    @pl.loop(0, chunks)
    def _(c):
        own_copy(c).start()

    for k in range(W_SLOTS):
        for cp in w_copies(k):
            cp.start()
    for k in range(D_SLOTS):
        for cp in wd_copies(k):
            cp.start()
    res_copy.start()

    row = lax.broadcasted_iota(jnp.int32, (rows, 1), 0)
    place, rest = row // BLOCK_SLOTS, row % BLOCK_SLOTS
    block, slot = rest // CAP, rest % CAP
    for m in range(2):
        dz, dy = offset(m, place)
        pair = ((z + dz) % 4) * 4 + (y + dy) % 4
        wanted = (2 * pair + x // 2) * CAP + slot
        for b in range(4):
            at = slice(b * tokens, (b + 1) * tokens)
            key = jnp.where(block == b, wanted, -1).astype(f32)
            first = packs_ref[b, 0:1, :] == key
            second = packs_ref[b, 1:2, :] == key
            spread[m, :, at] = jnp.where(first | second, 1.0, 0.0).astype(bf)
            weight = jnp.where(first, packs_ref[b, 2:3, :], 0.0) + jnp.where(second, packs_ref[b, 3:4, :], 0.0)
            merge[m, at, :] = weight.T.astype(bf)

    acc_g[...] = jnp.zeros_like(acc_g)
    acc_u[...] = jnp.zeros_like(acc_u)

    def pass_on(c):
        for i in range(2):
            near_copy(c, 1 - i).wait_recv()
            pass_copy(c, i).start()

        @pl.when(c + 2 < chunks)
        def _():
            for i in range(2):
                near_copy(c + 2, i).start()

    pass_on(0)

    @pl.loop(0, chunks + 2)
    def _(step):
        @pl.when(step + 1 < chunks)
        def _():
            pass_on(step + 1)

        @pl.when(step < chunks)
        def _():
            c = step
            own_copy(c).wait()
            for i in range(2):
                pass_copy(c, i).wait_recv()
            lines = tok[c].reshape(4 * tokens, F)

            @pl.loop(0, 2)
            def _(m):
                @pl.when(jnp.logical_not(shared(c)) | (m == mine))
                def _():
                    send[c, m] = jnp.dot(spread[m], lines, preferred_element_type=f32).astype(bf)

            seat_copies(c, 0, start)

            @pl.when(jnp.logical_not(shared(c)) | (mine == 0))
            def _():
                recv[c, 0, seat(0)] = send[c, 0, seat(0)]

        @pl.when(step >= 3)
        def _():
            k = step - 3
            s = k % W_SLOTS
            for cp in w_copies(k):
                cp.wait()

            @pl.when(shared(k))
            def _():
                mate_rows(k).wait_recv()

            @pl.when(jnp.logical_not(shared(k)))
            def _():
                for m, i in order:
                    seat_copy(k, m, i, recv, d_s, d_r, 1).wait_recv()

            @pl.loop(0, 2)
            def _(m):
                lines = recv[k, m]
                acc_g[m] += jnp.dot(lines, wg[s], preferred_element_type=f32)
                acc_u[m] += jnp.dot(lines, wu[s], preferred_element_type=f32)

            @pl.when(k + W_SLOTS < chunks)
            def _():
                for cp in w_copies(k + W_SLOTS):
                    cp.start()

        @pl.when((step >= 2) & shared(step - 2))
        def _():
            k = step - 2
            for i in SET_ORDER:
                seat_copy(k, mine, i, recv, d_s, d_r, 1).wait_recv()

            @pl.when(mine == 1)
            def _():
                seat_copy(k, mine, 0, recv, d_s, d_r, 1).wait_recv()

            mate_rows(k).start()

    last = chunks - 1
    for cp in w_copies(last) + wd_copies(0):
        cp.wait()
    seat_copies(last, 0, wait_recv)
    seat_copies(0, 0, wait_send)
    res_copy.wait()

    @pl.loop(0, 2)
    def _(m):
        lines = recv[last, m]
        acc_g[m] += jnp.dot(lines, wg[last % W_SLOTS], preferred_element_type=f32)
        acc_u[m] += jnp.dot(lines, wu[last % W_SLOTS], preferred_element_type=f32)

        @pl.loop(0, rows // 64)
        def _(t):
            at = pl.ds(pl.multiple_of(t * 64, 64), 64)
            g = acc_g[m, at, :]
            act[m, at, :] = (g / (1.0 + jnp.exp(-g)) * acc_u[m, at, :]).astype(bf)

        send[0, m] = jnp.dot(act[m], wd[0], preferred_element_type=f32).astype(bf)
        for i in SET_ORDER:
            seat_copy(0, m, i, back, r_s, r_r, -1).start()

        @pl.when(m == 1)
        def _():
            seat_copy(0, m, 0, back, r_s, r_r, -1).start()

        @pl.when(m == 0)
        def _():
            back[0, 0, seat(0)] = send[0, 0, seat(0)]

    def part(k, b):
        at = pl.ds(pl.multiple_of(b * tokens, tokens), tokens)
        part_ref[...] = jnp.dot(merge[mine, at, :], back[k, mine], preferred_element_type=f32)

        @pl.when(jnp.logical_not(shared(k)))
        def _():
            part_ref[...] += jnp.dot(merge[1 - mine, at, :], back[k, 1 - mine], preferred_element_type=f32)

        return part_ref[...]

    @pl.loop(0, chunks + 6)
    def _(step):
        @pl.when((step >= 1) & (step < chunks))
        def _():
            c = step
            s = c % D_SLOTS
            for cp in wd_copies(c):
                cp.wait()
            seat_copies(c, 0, wait_send)

            @pl.loop(0, 2)
            def _(m):
                @pl.when(jnp.logical_not(shared(c)) | (m != mine))
                def _():
                    send[c, m] = jnp.dot(act[m], wd[s], preferred_element_type=f32).astype(bf)

            @pl.when(shared(c))
            def _():
                mate_sums(c).start()

            @pl.when(jnp.logical_not(shared(c)))
            def _():
                for m, i in by_core:
                    seat_copy(c, m, i, back, r_s, r_r, -1).start()
                back[c, 0, seat(0)] = send[c, 0, seat(0)]

        @pl.when((step >= 1) & (step < chunks + 1))
        def _():
            k = step - 1

            @pl.when(shared(k))
            def _():
                mate_sums(k).wait_recv()
                both = jnp.dot(act[mine], wd[k % D_SLOTS], preferred_element_type=f32) + mate[k // 2].astype(f32)
                send[k, mine] = both.astype(bf)
                for i in SET_ORDER:
                    seat_copy(k, mine, i, back, r_s, r_r, -1).start()

                @pl.when(mine == 1)
                def _():
                    seat_copy(k, mine, 0, back, r_s, r_r, -1).start()

                @pl.when(mine == 0)
                def _():
                    back[k, 0, seat(0)] = send[k, 0, seat(0)]

            @pl.when(k + D_SLOTS < chunks)
            def _():
                for cp in wd_copies(k + D_SLOTS):
                    cp.start()

        @pl.when((step >= 3) & (step < chunks + 3))
        def _():
            k = step - 3
            seat_copies(k, 1, wait_recv)
            for i in range(2):
                pass_copy(k, i).wait_send()
            tok[k, 0] = part(k, (x + 2) % 4).astype(bf)
            for i in range(2):
                turn_copy(k, i).start()

        @pl.when((step >= 4) & (step < chunks + 4))
        def _():
            k = step - 4
            for i in range(2):
                near = slice(i * H, (i + 1) * H)
                rest = slice((1 - i) * H, (2 - i) * H)
                side = part(k, (x + (3, 1)[i]) % 4)
                turn_copy(k, i).wait_recv()
                tok[k, 1 + i, :, near] = (side[:, near] + turn_in[k, i].astype(f32)).astype(bf)
                tok[k, 1 + i, :, rest] = side[:, rest].astype(bf)
                side_copy(k, i).start()

        @pl.when(step >= 6)
        def _():
            k = step - 6
            total = part(k, x)
            for i in range(2):
                side_copy(k, i).wait_recv()
                total = total + side_in[k, i].astype(f32)
            out_ref[:, cols(k)] = (res_ref[:, cols(k)] + mod_ref[3:4, cols(k)] * total).astype(out_ref.dtype)

    @pl.loop(0, chunks)
    def _(c):
        for i in range(2):
            near_copy(c, i).wait_send()
            turn_copy(c, i).wait_send()
            side_copy(c, i).wait_send()
        seat_copies(c, 1, wait_send)

        @pl.when(shared(c))
        def _():
            mate_rows(c).wait_send()
            mate_sums(c).wait_send()


def experts(moe_in, residual, modulation, packs, weights):
    tokens, width = moe_in.shape
    chunks = 8
    F = width // chunks
    rows = 8 * BLOCK_SLOTS
    hidden = 2 * weights[0].shape[1]
    bf, f32 = jnp.bfloat16, jnp.float32
    dma = pltpu.SemaphoreType.DMA
    vmem = pl.BlockSpec(memory_space=pltpu.VMEM)
    hbm = pl.BlockSpec(memory_space=pl.ANY)
    return pl.pallas_call(
        functools.partial(expert_kernel, chunks),
        out_shape=jax.ShapeDtypeStruct((tokens, width), bf),
        in_specs=[hbm] * 2 + [vmem] * 2 + [hbm] * 6,
        out_specs=vmem,
        scratch_shapes=[
            pltpu.VMEM((chunks, 4, tokens, F), bf),
            pltpu.VMEM((chunks, 2, rows, F), bf),
            pltpu.VMEM((chunks, 2, rows, F), bf),
            pltpu.VMEM((chunks, 2, rows, F), bf),
            pltpu.VMEM((SHARED, rows, F), bf),
            pltpu.VMEM((chunks, 2, tokens, F // 2), bf),
            pltpu.VMEM((chunks, 2, tokens, F), bf),
            pltpu.VMEM((2, rows, hidden), f32),
            pltpu.VMEM((2, rows, hidden), f32),
            pltpu.VMEM((2, rows, hidden), bf),
            pltpu.VMEM((W_SLOTS, F, hidden), bf),
            pltpu.VMEM((W_SLOTS, F, hidden), bf),
            pltpu.VMEM((D_SLOTS, hidden, F), bf),
            pltpu.VMEM((2, rows, 4 * tokens), bf),
            pltpu.VMEM((2, 4 * tokens, rows), bf),
            pltpu.VMEM((tokens, F), f32),
            pltpu.VMEM((tokens, width), f32),
        ]
        + [dma((chunks, 2))] * 4
        + [dma((chunks, 16))] * 4
        + [dma((chunks,))] * 4
        + [dma((chunks, 2))] * 4
        + [dma((W_SLOTS, 4)), dma((D_SLOTS, 2)), dma((chunks,)), dma],
        compiler_params=pltpu.CompilerParams(
            collective_id=0, has_side_effects=True, vmem_limit_bytes=62 * 1024 * 1024
        ),
        cost_estimate=pl.CostEstimate(flops=26_000_000_000, bytes_accessed=40_000_000, transcendentals=800_000),
        name="experts",
    )(moe_in, residual, modulation, packs, *weights)


def local(
    latent,
    attention_in,
    out_weight,
    modulation,
    route_experts,
    route_slots,
    route_gates,
    gate_weight,
    up_weight,
    down_weight,
):
    weights = [gate_weight[0], up_weight[0], down_weight[0]]
    routes = [route_experts[0].T, route_slots[0].T, route_gates[0].T]
    qkv = jnp.transpose(attention_in[0], (1, 0, 2))
    moe_in, residual, packs, far = attention(qkv, latent[0], out_weight, modulation, routes, weights)
    both = [w for pair in zip(weights, far) for w in pair]
    return experts(moe_in, residual, modulation, packs, both)[None]


def solution(mesh):
    return jax.shard_map(
        local,
        mesh=mesh,
        in_specs=(
            P("ep", "sp", None),
            P("ep", "sp", None, None),
            P("sp", None),
            P(),
            P("ep", "sp", None),
            P("ep", "sp", None),
            P("ep", "sp", None),
            P("ep", None, "sp"),
            P("ep", None, "sp"),
            P("ep", "sp", None),
        ),
        out_specs=P("ep", "sp", None),
        check_vma=False,
    )
```
